32 devices in a mesh: ctx: 8 (over z, y), wt: 4 (over x, core).
Axes of the slice: x: 2, y: 2, z: 4, core: 2. Of those that a mesh axis runs over, the one named last changes fastest.
Arguments:
- tokens: bfloat16 [2, 4, 3072, 2560], P(None, 'wt', 'ctx'), may hold values from -6 to 6
- segment_ids: int32 [2, 4, 3072], P(None, 'wt', 'ctx'), may hold values from 0 to 3, never falling along the last dimension, each value on 1 to 2304 neighbouring positions
- cotangent: bfloat16 [2, 4, 3072, 2560], P(None, 'wt', 'ctx'), may hold values from -6 to 6
- gain_attn: bfloat16 [2560], P(('ctx', 'wt')), may hold values from 0.5 to 1.5
- w_query: bfloat16 [2560, 2560], P(('ctx', 'wt')), may hold values from -0.125 to 0.125
- w_key: bfloat16 [2560, 256], P(('ctx', 'wt')), may hold values from -0.125 to 0.125
- w_value: bfloat16 [2560, 256], P(('ctx', 'wt')), may hold values from -0.125 to 0.125
- w_out: bfloat16 [2560, 2560], P(None, ('ctx', 'wt')), may hold values from -1 to 1
- gain_mlp: bfloat16 [2560], P(('ctx', 'wt')), may hold values from 0.5 to 1.5
- w_gate: bfloat16 [2560, 7680], P('ctx', 'wt'), may hold values from -0.125 to 0.125
- w_up: bfloat16 [2560, 7680], P('ctx', 'wt'), may hold values from -0.125 to 0.125
- w_down: bfloat16 [7680, 2560], P('wt', 'ctx'), may hold values from -0.0625 to 0.0625
Outputs:
- output: float32 [2, 4, 3072, 2560], P(None, 'wt', 'ctx')
- grad_tokens: float32 [2, 4, 3072, 2560], P(None, 'wt', 'ctx')
- grad_gain_attn: float32 [2560], P(('ctx', 'wt'))
- grad_w_query: float32 [2560, 2560], P(('ctx', 'wt'))
- grad_w_key: float32 [2560, 256], P(('ctx', 'wt'))
- grad_w_value: float32 [2560, 256], P(('ctx', 'wt'))
- grad_w_out: float32 [2560, 2560], P(None, ('ctx', 'wt'))
- grad_gain_mlp: float32 [2560], P(('ctx', 'wt'))
- grad_w_gate: float32 [2560, 7680], P('ctx', 'wt')
- grad_w_up: float32 [2560, 7680], P('ctx', 'wt')
- grad_w_down: float32 [7680, 2560], P('wt', 'ctx')
The draws below stay inside these ranges and needn't reach their ends.
Inputs may be any that keep to these rules, and one draw needn't show every extreme that they name: `segment_ids`: along each sequence the ids never fall and run through all 4 documents; each document has 1 to 2304 tokens and one has exactly that many.
All inputs are finite; a program needn't handle non-finite values.
Results may differ from the reference program's by a relative error of at most 0.017.
Values may be sent and summed in bfloat16 or wider, within the bound.
No kernel may reach another device: no remote copies, remote signals or barrier semaphores. Data moves between devices by JAX's collectives and lax.ppermute only.
A program may use at most 512 MiB of HBM per device.

```python
import math
import jax
import jax.numpy as jnp
import numpy as np
from jax import lax

D = 2560
H = 10
DH = 256
FF = 7680
WINDOW = 2048
SEQ_LEN = 3072
DOCS = 4
MICRO = 2
SEQS = 4


def raised(drawn, stream_key, source, target, blocks, factor):
    owner, partner = [(jnp.arange(drawn.shape[axis_at]) // (drawn.shape[axis_at] // blocks)).reshape([-1 if axis == axis_at else 1 for axis in range(drawn.ndim)]) for axis_at in (source, target)]
    chosen = jax.random.permutation(stream_key, blocks)[partner]
    strong = (owner == chosen) | (owner == (partner + blocks // 2) % blocks)
    return jnp.where(strong, factor * drawn, drawn)


def levels(stream_key, extent, split, low, high):
    def one(dim, shards_of):
        draws = jax.random.uniform(jax.random.fold_in(jax.random.fold_in(stream_key, 6), dim), (shards_of,), jnp.float32, low / len(split), high / len(split))
        return jnp.repeat(jnp.exp(draws), extent[dim] // shards_of).reshape((-1,) + (1,) * (len(extent) - dim - 1))

    factor_of = one(*split[0])
    for cut in split[1:]:
        factor_of = factor_of * one(*cut)
    return factor_of


def profile(number_of, total, limit, slope):
    weights = [(1 << 20) // math.isqrt(grade ** slope) + 1 for grade in range(2, number_of + 1)]
    rest, given = total - limit - (number_of - 1), [1] * (number_of - 1)
    while rest > 0:
        free = [i for i in range(number_of - 1) if given[i] < limit]
        pool, remaining = sum([weights[i] for i in free]), rest
        for i in free:
            addition = min(limit - given[i], max(1, remaining * weights[i] // pool), rest)
            given[i] = given[i] + addition
            rest = rest - addition
    return np.array([limit] + given)


def uneven(own_key, count, total, reach, lean):
    if count == 2:
        one = jax.random.randint(own_key, (), max(1, total - reach), min(reach, total - 1) + 1)
        return jnp.stack([one, total - one])
    lengths = jnp.asarray(profile(count, total, reach, lean), jnp.int32)
    pairs = (count - 1) // 2
    source_of, taker = lengths[1:1 + 2 * pairs:2], lengths[2:2 + 2 * pairs:2]
    margin = jnp.minimum(source_of - 1, reach - taker)
    passed = jax.random.randint(jax.random.fold_in(own_key, 1), (pairs,), 0, 1 << 20) % (margin + 1)
    lengths = lengths.at[1:1 + 2 * pairs:2].set(source_of - passed).at[2:2 + 2 * pairs:2].set(taker + passed)
    return lengths[jax.random.permutation(jax.random.fold_in(own_key, 2), count)]


def gaussian(rng, dims, width, most, pieces=(), held_as=jnp.bfloat16):
    drawn = jax.random.normal(rng, dims, jnp.float32) * width
    if len(pieces) > 0:
        drawn = levels(rng, dims, pieces, -0.22, 0.18) * drawn
    return jnp.clip(drawn, min=-most, max=most).astype(held_as)


def heavy_noise(key, shape, deviation, most, cuts, heavy, held_as=jnp.bfloat16):
    result = deviation * jax.random.normal(key, shape, jnp.float32)
    if cuts:
        result = result * levels(key, shape, cuts, -0.22, 0.18)
    return jnp.clip(raised(result, jax.random.fold_in(key, 3), *heavy), -most, most).astype(held_as)


def setup_inputs(seed: int = 0) -> dict:
    keys = jax.random.split(jax.random.key(seed), 13)
    return {
        "tokens": gaussian(keys[0], (MICRO, SEQS, SEQ_LEN, D), 1.0, 6.0, ((1, 4), (2, 8))),
        "segment_ids": jax.vmap(lambda own: jnp.searchsorted(jnp.cumsum(uneven(own, DOCS, SEQ_LEN, SEQ_LEN * 3 // 4, 0)), jnp.arange(SEQ_LEN), side="right"))(jax.random.split(keys[1], MICRO * SEQS)).reshape((MICRO, SEQS, SEQ_LEN)).astype(jnp.int32),
        "cotangent": heavy_noise(keys[2], (MICRO, SEQS, SEQ_LEN, D), 1.0, 6.0, ((1, 4), (2, 8)), (2, 3, 8, 2.0)),
        "gain_attn": jnp.clip(1.0 + 0.1 * jax.random.normal(keys[3], (D,), jnp.float32), 0.5, 1.5).astype(jnp.bfloat16),
        "w_query": gaussian(keys[4], (D, H * DH), D ** -0.5, 0.125, ((0, 32),)),
        "w_key": gaussian(keys[5], (D, DH), D ** -0.5, 0.125, ((0, 32),)),
        "w_value": gaussian(keys[6], (D, DH), D ** -0.5, 0.125, ((0, 32),)),
        "w_out": gaussian(keys[7], (H * DH, D), (max(1, H * DH // 64)) ** -0.5, 1.0, ((1, 32),)),
        "gain_mlp": jnp.clip(1.0 + 0.1 * jax.random.normal(keys[8], (D,), jnp.float32), 0.5, 1.5).astype(jnp.bfloat16),
        "w_gate": gaussian(keys[9], (D, FF), D ** -0.5, 0.125, ((0, 8), (1, 4))),
        "w_up": gaussian(keys[10], (D, FF), D ** -0.5, 0.125, ((0, 8), (1, 4))),
        "w_down": gaussian(keys[11], (FF, D), FF ** -0.5, 0.0625, ((0, 4), (1, 8))),
    }


@jax.custom_vjp
def low(v):
    return lax.optimization_barrier(v.astype(jnp.bfloat16)).astype(jnp.float32)

@jax.custom_vjp
def low_back(v):
    return v

def low_keep(v):
    return (low(v), None)

def low_pass(kept, grad):
    return (grad,)

def back_keep(v):
    return (v, None)

def back_low(kept, grad):
    return (low(grad),)
low.defvjp(low_keep, low_pass)
low_back.defvjp(back_keep, back_low)
EPSILON = 1e-06
NEGATIVE = -1e+30
HIGHEST = lax.Precision.HIGHEST

def matmul(left, right):
    return jnp.dot(left, right, precision=HIGHEST)

def rms_scale(values, gain):
    return values * lax.rsqrt(lax.optimization_barrier(jnp.mean(values * values, axis=-1, keepdims=True)) + EPSILON) * gain

def doc_positions(doc_ids):
    index = jnp.arange(doc_ids.shape[0], dtype=jnp.int32)
    starts = jnp.concatenate([jnp.ones((1,), dtype=jnp.bool_), doc_ids[1:] != doc_ids[:-1]])
    first = lax.cummax(jnp.where(starts, index, 0), axis=0)
    return index - first

def rope_tables(positions, half_size):
    freqs = 10000.0 ** (-jnp.arange(half_size, dtype=jnp.float32) / half_size)
    angles = positions.astype(jnp.float32)[:, None] * freqs[None, :]
    return (jnp.cos(angles), jnp.sin(angles))

def rotate(values, cosine_table, sine_table):
    half_size = values.shape[-1] // 2
    first_half = values[..., :half_size]
    second_half = values[..., half_size:]
    return jnp.concatenate([first_half * cosine_table - second_half * sine_table, second_half * cosine_table + first_half * sine_table], axis=-1)

def block_forward(inputs, doc_ids, gain_attn, w_query, w_key, w_value, w_out, gain_mlp, w_gate, w_up, w_down):
    length = inputs.shape[0]
    cosine_table, sine_table = rope_tables(doc_positions(doc_ids), DH // 2)
    normed = low(rms_scale(inputs, gain_attn))
    queries = low_back(matmul(normed, w_query)).reshape(length, H, DH)
    queries = low(rotate(queries, cosine_table[:, None, :], sine_table[:, None, :]) * DH ** (-0.5))
    key_sent = low(low_back(matmul(normed, w_key)))
    key_rot = low(rotate(key_sent, cosine_table, sine_table))
    value_rows = low(low_back(matmul(normed, w_value)))
    key_index = jnp.arange(length, dtype=jnp.int32)
    block_rows = min(512, length)

    def attend(row_start):
        query_block = lax.dynamic_slice_in_dim(queries, row_start, block_rows, 0)
        query_ids = lax.dynamic_slice_in_dim(doc_ids, row_start, block_rows, 0)
        distance = (row_start + jnp.arange(block_rows, dtype=jnp.int32))[:, None] - key_index[None, :]
        visible = (query_ids[:, None] == doc_ids[None, :]) & (distance >= 0) & (distance < WINDOW)
        scores = jnp.einsum('rhd,kd->hrk', query_block, key_rot, precision=HIGHEST)
        scores = low_back(jnp.where(visible[None], scores, NEGATIVE))
        attn_probs = low(jax.nn.softmax(scores, axis=-1))
        mixture = jnp.einsum('hrk,kd->rhd', attn_probs, value_rows, precision=HIGHEST)
        return mixture.reshape(block_rows, H * DH)
    starts = jnp.arange(length // block_rows, dtype=jnp.int32) * block_rows
    attended = lax.map(jax.checkpoint(attend), starts).reshape(length, H * DH)
    attended = low(low_back(attended))
    branch = low_back(matmul(attended, w_out))
    middle = inputs + branch
    normed_mlp = low(rms_scale(middle, gain_mlp))
    gate_rows = low_back(matmul(normed_mlp, w_gate))
    up_rows = low_back(matmul(normed_mlp, w_up))
    hidden = low(jax.nn.gelu(gate_rows) * up_rows)
    return middle + low_back(matmul(hidden, w_down))

def reference(tokens, segment_ids, cotangent, gain_attn, w_query, w_key, w_value, w_out, gain_mlp, w_gate, w_up, w_down):
    params = tuple((weight.astype(jnp.float32) for weight in (gain_attn, w_query, w_key, w_value, w_out, gain_mlp, w_gate, w_up, w_down)))
    sequences = tokens.reshape(MICRO * SEQS, SEQ_LEN, D).astype(jnp.float32)
    doc_rows = segment_ids.reshape(MICRO * SEQS, SEQ_LEN).astype(jnp.int32)
    cot_rows = cotangent.reshape(MICRO * SEQS, SEQ_LEN, D).astype(jnp.float32)

    def one_sequence(totals, sliced):
        inputs, doc_ids, cot_seq = sliced

        def forward(inputs_f, *weights):
            return block_forward(inputs_f, doc_ids, *weights)
        outputs, backward = jax.vjp(forward, inputs, *params)
        gradients = backward(cot_seq)
        totals = tuple((running + update for running, update in zip(totals, gradients[1:])))
        return (totals, (outputs, gradients[0]))
    zeros_init = tuple((jnp.zeros_like(weight) for weight in params))
    totals, (outputs, input_grads) = lax.scan(one_sequence, zeros_init, (sequences, doc_rows, cot_rows))
    return (outputs.reshape(MICRO, SEQS, SEQ_LEN, D), input_grads.reshape(MICRO, SEQS, SEQ_LEN, D), totals[0], totals[1], totals[2], totals[3], totals[4], totals[5], totals[6], totals[7], totals[8])
```

```python
import functools
import math

import jax
import jax.numpy as jnp
from jax import lax
from jax.experimental import pallas as pl
from jax.experimental.pallas import tpu as pltpu
from jax.sharding import PartitionSpec as P

WINDOW = 2048
EPSILON = 1e-06
NEGATIVE = -1e30
LOG2E = math.log2(math.e)
LN2 = math.log(2.0)
F32 = jnp.float32
BF16 = jnp.bfloat16


def rms_scale(values, gain):
    return values * lax.rsqrt(jnp.mean(values * values, axis=-1, keepdims=True) + EPSILON) * gain


def dot(left, right, out=F32):
    return jnp.dot(left, right, preferred_element_type=out)


def contract_rows(left, right, out=F32):
    return lax.dot_general(left, right, (((0,), (0,)), ((), ())), preferred_element_type=out)


def contract_last(left, right, out=F32):
    return lax.dot_general(left, right, (((1,), (1,)), ((), ())), preferred_element_type=out)


def ring_order(count):
    return list(range(0, count, 2)) + [i for i in range(count - 1, 0, -1) if i % 2]


def ring_step(block, shift):
    count = lax.axis_size("ctx")
    order = ring_order(count)
    return lax.ppermute(
        block, "ctx", [(order[i], order[(i + shift) % count]) for i in range(count)]
    )


def ring_index(offset):
    count = lax.axis_size("ctx")
    order = ring_order(count)
    place = [order.index(i) for i in range(count)]
    here = jnp.asarray(place, jnp.int32)[lax.axis_index("ctx")]
    return jnp.asarray(order, jnp.int32)[(here + offset) % count]


def ring_gather(block):
    count = lax.axis_size("ctx")
    half = count // 2
    cut = block.shape[0] // 2 // 8 * 8
    found = jnp.zeros((count,) + block.shape, block.dtype)

    def put(found, piece, offset, row):
        start = (ring_index(offset), row) + (0,) * (block.ndim - 1)
        return lax.dynamic_update_slice(found, piece[None], start)

    found = put(found, block, 0, 0)
    ahead = behind = block
    for step in range(1, half):
        ahead = ring_step(ahead, 1)
        behind = ring_step(behind, -1)
        found = put(found, ahead, -step, 0)
        found = put(found, behind, step, 0)
    low = ring_step(ahead[:cut], 1)
    high = ring_step(behind[cut:], -1)
    found = put(found, low, half, 0)
    found = put(found, high, half, cut)
    return found


def ring_scatter(terms):
    count = terms.shape[0]
    half = count // 2
    cut = terms.shape[1] // 2 // 8 * 8

    def own(offset):
        return lax.dynamic_index_in_dim(terms, ring_index(offset), 0, keepdims=False)

    def add(first, second):
        return (first.astype(F32) + second.astype(F32)).astype(BF16)

    far = own(half)
    ahead = ring_step(far[:cut], 1)
    behind = ring_step(far[cut:], -1)
    if half == 1:
        return own(0).astype(F32) + jnp.concatenate([ahead, behind], axis=0).astype(F32)
    for step in range(half - 1, 0, -1):
        up, down = own(step), own(-step)
        if step == half - 1:
            up = jnp.concatenate([add(up[:cut], ahead), up[cut:]], axis=0)
            down = jnp.concatenate([down[:cut], add(down[cut:], behind)], axis=0)
        else:
            up, down = add(up, ahead), add(down, behind)
        ahead = ring_step(up, 1)
        behind = ring_step(down, -1)
    return own(0).astype(F32) + ahead.astype(F32) + behind.astype(F32)


def wt_swap(block, bit):
    count = lax.axis_size("wt")
    return lax.ppermute(block, "wt", [(i, i ^ bit) for i in range(count)])


def core_swap(block):
    return wt_swap(block, 1)


def x_swap(block):
    return wt_swap(block, 2)


def gather_everywhere(block):
    here = lax.axis_index("wt")
    rows, width = block.shape
    mine = ring_gather(block)
    far = x_swap(mine)
    found = jnp.zeros((mine.shape[0], 4, rows, width), block.dtype)
    for piece, bit in ((mine, 0), (far, 2), (core_swap(mine), 1), (core_swap(far), 3)):
        found = lax.dynamic_update_slice(found, piece[:, None], (0, here ^ bit, 0, 0))
    return found.reshape(-1, width)


def scatter_everywhere(terms):
    here = lax.axis_index("wt")
    count = lax.axis_size("ctx")
    rows = terms.shape[0] // (4 * count)
    split = terms.reshape(count, 2, 2, rows, terms.shape[1])
    x_here, core_here = here // 2, here % 2
    kept = lax.dynamic_index_in_dim(split, core_here, 2, keepdims=False)
    sent = lax.dynamic_index_in_dim(split, 1 - core_here, 2, keepdims=False)
    both = (kept.astype(F32) + core_swap(sent).astype(F32)).astype(BF16)
    kept = lax.dynamic_index_in_dim(both, x_here, 1, keepdims=False)
    sent = lax.dynamic_index_in_dim(both, 1 - x_here, 1, keepdims=False)
    return ring_scatter((kept.astype(F32) + x_swap(sent).astype(F32)).astype(BF16))


def gather_wt(block):
    chip = jnp.concatenate([block, x_swap(block)], axis=0)
    return jnp.concatenate([chip, core_swap(chip)], axis=0)


def scatter_wt(terms):
    rows = terms.shape[0] // 4
    other = core_swap(terms[2 * rows :])
    far = (terms[rows : 2 * rows].astype(F32) + other[rows:].astype(F32)).astype(BF16)
    near = terms[:rows].astype(F32) + other[:rows].astype(F32)
    return near + x_swap(far).astype(F32)


def rotate(values, cosine, sine):
    half = values.shape[-1] // 2
    first, second = values[:, :half], values[:, half:]
    return jnp.concatenate(
        [first * cosine - second * sine, second * cosine + first * sine], axis=-1
    )


def visible(start, keys, low, high):
    index = start + lax.broadcasted_iota(jnp.int32, (keys, low.shape[1]), 0)
    return (index >= low) & (index <= high)


def attend_kernel(
    spans, q_ref, kv_ref, low_ref, high_ref, cos_ref, sin_ref,
    out_ref, qrot_ref, lse_ref, vt_ref, *, heads, size, keys,
):
    rows = q_ref.shape[0]
    scale = size ** -0.5 * LOG2E

    @pl.when(pl.program_id(0) == 0)
    def _():
        vt_ref[...] = kv_ref[:, size:].T

    turned = []
    for head in range(heads):
        part = rotate(q_ref[:, head * size : (head + 1) * size], cos_ref[...], sin_ref[...])
        part = (part * scale).astype(BF16)
        qrot_ref[:, head * size : (head + 1) * size] = part
        turned.append(part.T)
    qt = jnp.concatenate(turned, axis=1)
    low, high = low_ref[...], high_ref[...]

    def step(block, carry, masked):
        top, total, acc = carry
        start = pl.multiple_of(block * keys, keys)
        scores = dot(kv_ref[pl.ds(start, keys), :size], qt)
        if masked:
            scores = jnp.where(visible(start, keys, low, high), scores, NEGATIVE)
        new_top = jnp.maximum(top, jnp.max(scores, axis=0, keepdims=True))
        probs = jnp.exp2(scores - new_top)
        fade = jnp.exp2(top - new_top)
        total = total * fade + jnp.sum(probs, axis=0, keepdims=True)
        acc = acc * fade + dot(vt_ref[:, pl.ds(start, keys)], probs.astype(BF16))
        return new_top, total, acc

    carry = (
        jnp.full((1, heads * rows), NEGATIVE, F32),
        jnp.zeros((1, heads * rows), F32),
        jnp.zeros((size, heads * rows), F32),
    )
    carry = lax.fori_loop(spans[0], spans[1], functools.partial(step, masked=True), carry)
    carry = lax.fori_loop(spans[2], spans[3], functools.partial(step, masked=False), carry)
    carry = lax.fori_loop(spans[4], spans[5], functools.partial(step, masked=True), carry)
    top, total, acc = carry
    acc = acc * (1.0 / total)
    lse_ref[0] = top + jnp.log2(total)
    for head in range(heads):
        out_ref[:, head * size : (head + 1) * size] = (
            acc[:, head * rows : (head + 1) * rows].astype(BF16).T
        )


def attend_back_kernel(
    spans, q_ref, kv_ref, low_ref, high_ref, cos_ref, sin_ref, out_ref, grad_ref, lse_ref,
    dq_ref, dkv_ref, kt_ref, dk_ref, dv_ref, *, heads, size, keys,
):
    rows = q_ref.shape[0]

    @pl.when(pl.program_id(0) == 0)
    def _():
        kt_ref[...] = kv_ref[:, :size].T
        dk_ref[...] = jnp.zeros_like(dk_ref)
        dv_ref[...] = jnp.zeros_like(dv_ref)

    parts = [slice(head * size, (head + 1) * size) for head in range(heads)]
    q = jnp.concatenate([q_ref[:, part] for part in parts], axis=0)
    grad = jnp.concatenate([grad_ref[:, part] for part in parts], axis=0)
    out_t = jnp.concatenate([out_ref[:, part].T for part in parts], axis=1)
    qt, grad_t = q.T, grad.T
    delta = jnp.sum(grad_t.astype(F32) * out_t.astype(F32), axis=0, keepdims=True)
    low, high, lse = low_ref[...], high_ref[...], lse_ref[0]

    def step(block, dq, masked):
        start = pl.multiple_of(block * keys, keys)
        here = pl.ds(start, keys)
        scores = dot(kv_ref[here, :size], qt)
        if masked:
            scores = jnp.where(visible(start, keys, low, high), scores, NEGATIVE)
        probs = jnp.exp2(scores - lse)
        probs_grad = dot(kv_ref[here, size:], grad_t)
        score_grad = (probs * (probs_grad - delta)).astype(BF16)
        dv_ref[here, :] += dot(probs.astype(BF16), grad)
        dk_ref[here, :] += dot(score_grad, q)
        return dq + dot(kt_ref[:, here], score_grad)

    dq = jnp.zeros((size, heads * rows), F32)
    dq = lax.fori_loop(spans[0], spans[1], functools.partial(step, masked=True), dq)
    dq = lax.fori_loop(spans[2], spans[3], functools.partial(step, masked=False), dq)
    dq = lax.fori_loop(spans[4], spans[5], functools.partial(step, masked=True), dq)
    for head, part in enumerate(parts):
        turned = rotate(dq[:, head * rows : (head + 1) * rows].T, cos_ref[...], -sin_ref[...])
        dq_ref[:, part] = (turned * size ** -0.5).astype(BF16)

    @pl.when(pl.program_id(0) == pl.num_programs(0) - 1)
    def _():
        dkv_ref[:, :size] = (dk_ref[...] * LN2).astype(BF16)
        dkv_ref[:, size:] = dv_ref[...].astype(BF16)


def attention_calls(rows, width, size, total, keys):
    heads = 2 if (width // size) % 2 == 0 else 1
    groups = width // size // heads
    span = heads * size
    head_block = pl.BlockSpec((rows, span), lambda g, s: (0, g))

    def whole(*shape):
        return pl.BlockSpec(shape, lambda g, s: (0,) * len(shape))

    lse_block = pl.BlockSpec((1, 1, heads * rows), lambda g, s: (g, 0, 0))
    shared = [
        head_block, whole(total, 2 * size), whole(1, heads * rows), whole(1, heads * rows),
        whole(rows, size // 2), whole(rows, size // 2),
    ]
    lse_shape = jax.ShapeDtypeStruct((groups, 1, heads * rows), F32)
    row_shape = jax.ShapeDtypeStruct((rows, width), BF16)
    params = pltpu.CompilerParams(vmem_limit_bytes=48 * 2**20)
    work = rows * width * min(total, WINDOW) * 2
    sizes = dict(heads=heads, size=size, keys=keys)
    forward = pl.pallas_call(
        functools.partial(attend_kernel, **sizes),
        out_shape=(row_shape, row_shape, lse_shape),
        grid_spec=pltpu.PrefetchScalarGridSpec(
            num_scalar_prefetch=1, grid=(groups,), in_specs=shared,
            out_specs=(head_block, head_block, lse_block),
            scratch_shapes=[pltpu.VMEM((size, total), BF16)],
        ),
        compiler_params=params,
        cost_estimate=pl.CostEstimate(
            flops=2 * work, bytes_accessed=rows * width * 8, transcendentals=work // size // 2
        ),
    )
    backward = pl.pallas_call(
        functools.partial(attend_back_kernel, **sizes),
        out_shape=(row_shape, jax.ShapeDtypeStruct((total, 2 * size), BF16)),
        grid_spec=pltpu.PrefetchScalarGridSpec(
            num_scalar_prefetch=1, grid=(groups,),
            in_specs=shared + [head_block, head_block, lse_block],
            out_specs=(head_block, whole(total, 2 * size)),
            scratch_shapes=[
                pltpu.VMEM((size, total), BF16),
                pltpu.VMEM((total, size), F32),
                pltpu.VMEM((total, size), F32),
            ],
        ),
        compiler_params=params,
        cost_estimate=pl.CostEstimate(
            flops=5 * work, bytes_accessed=rows * width * 10, transcendentals=work // size // 2
        ),
    )
    return forward, backward, heads


def pad_rows(array, rows):
    return jnp.pad(array, ((0, rows - array.shape[0]), (0, 0)))


def local(
    tokens, segment_ids, cotangent, gain_attn, w_query, w_key, w_value, w_out, gain_mlp,
    w_gate, w_up, w_down,
):
    micros, _, rows, width = tokens.shape
    size = w_key.shape[1]
    count = lax.axis_size("ctx")
    total = rows * count
    first = lax.axis_index("ctx") * rows
    padded = -(-rows // 128) * 128
    keys = min(384, total)
    forward, backward, heads = attention_calls(padded, w_query.shape[1], size, total, keys)

    ids = segment_ids[:, 0]
    ids_all = lax.all_gather(ids, "ctx", axis=1, tiled=True)

    gains = jnp.stack([gain_attn, gain_mlp], axis=1)
    narrow = jnp.concatenate([w_key, w_value, jnp.pad(gains, ((0, 0), (0, 126)))], axis=1)
    narrow = gather_everywhere(narrow)
    w_kv = narrow[:, : 2 * size]
    gain_first = narrow[:, 2 * size].astype(F32)
    gain_second = narrow[:, 2 * size + 1].astype(F32)
    query_full = gather_everywhere(w_query)
    out_full = gather_everywhere(w_out.T)

    index = first + jnp.arange(rows, dtype=jnp.int32)
    begins = jnp.sum(
        (ids_all[:, None, :] < ids[:, :, None]).astype(jnp.int32), axis=-1, dtype=jnp.int32
    )
    position = (index[None] - begins).astype(F32)
    half = size // 2
    freqs = 10000.0 ** (-jnp.arange(half, dtype=F32) / half)
    angles = position[:, :, None] * freqs
    cosine, sine = jnp.cos(angles), jnp.sin(angles)
    lowest = jnp.maximum(begins, index[None] - (WINDOW - 1))

    inputs = tokens[:, 0].astype(F32)
    normed = rms_scale(inputs, gain_first).astype(BF16).reshape(micros * rows, width)
    kv = dot(normed, w_kv, BF16).reshape(micros, rows, 2 * size)
    queries = dot(normed, query_full).reshape(micros, rows, -1)

    saved = []
    middles = []
    mlp_rows = []
    for m in range(micros):
        key_rot = rotate(kv[m, :, :size].astype(F32), cosine[m], sine[m]).astype(BF16)
        kv_all = ring_gather(jnp.concatenate([key_rot, kv[m, :, size:]], axis=1))
        kv_all = kv_all.reshape(total, 2 * size)
        full_from = (jnp.max(lowest[m]) + keys - 1) // keys
        full_to = (first + 1) // keys
        last = (first + rows - 1) // keys + 1
        spans = jnp.stack([
            jnp.min(lowest[m]) // keys, jnp.minimum(full_from, last),
            full_from, full_to,
            jnp.maximum(full_from, full_to), last,
        ]).astype(jnp.int32)

        def lanes(values):
            return jnp.tile(jnp.pad(values, (0, padded - rows))[None], (1, heads))

        shared = (
            kv_all, lanes(lowest[m]), lanes(index),
            pad_rows(cosine[m], padded), pad_rows(sine[m], padded),
        )
        attended, query_rot, lse = forward(spans, pad_rows(queries[m], padded), *shared)
        saved.append((spans, query_rot, shared, attended, lse))
        middle = inputs[m] + contract_last(attended[:rows], out_full)
        middles.append(middle)
        mlp_rows.append(rms_scale(middle, gain_second).astype(BF16))

    normed_all = gather_wt(jnp.concatenate(mlp_rows, axis=0))
    cot_all = gather_wt(cotangent.reshape(micros * rows, width))
    hidden_cols = w_gate.shape[1]
    gate_full = ring_gather(w_gate).reshape(width, hidden_cols)
    up_full = ring_gather(w_up).reshape(width, hidden_cols)
    down_full = ring_gather(w_down.T).reshape(width, hidden_cols)

    gate_rows = dot(normed_all, gate_full)
    up_rows = dot(normed_all, up_full)
    hidden = (jax.nn.gelu(gate_rows) * up_rows).astype(BF16)

    def scatter_weight(left, right):
        return ring_scatter(contract_rows(left, right, BF16).reshape(count, -1, hidden_cols))

    grad_down = scatter_weight(cot_all, hidden).T
    hidden_grad = dot(cot_all, down_full)
    gelu_gate, gelu_back = jax.vjp(jax.nn.gelu, gate_rows)
    gate_grad = gelu_back(hidden_grad * up_rows)[0].astype(BF16)
    up_grad = (hidden_grad * gelu_gate).astype(BF16)
    mlp_in_grad = scatter_wt(
        (contract_last(gate_grad, gate_full) + contract_last(up_grad, up_full)).astype(BF16)
    ).reshape(micros, rows, width)
    grad_gate = scatter_weight(normed_all, gate_grad)
    grad_up = scatter_weight(normed_all, up_grad)
    mlp_out = scatter_wt(contract_last(hidden, down_full, BF16)).reshape(micros, rows, width)
    output = jnp.stack(middles) + mlp_out

    middle_grads, query_grads, key_value_grads, branch_grads, gain_two = [], [], [], [], []
    for m in range(micros):
        spans, query_rot, shared, attended, lse = saved[m]
        norm_back = jax.vjp(rms_scale, middles[m], gain_second)[1]
        middle_part, gain_part = norm_back(mlp_in_grad[m])
        gain_two.append(gain_part)
        middle_grad = middle_part + cotangent[m, 0].astype(F32)
        middle_grads.append(middle_grad)
        branch_grad = middle_grad.astype(BF16)
        branch_grads.append(branch_grad)
        attended_grad = dot(branch_grad, out_full, BF16)
        query_grad, kv_term = backward(
            spans, query_rot, *shared, attended, pad_rows(attended_grad, padded), lse
        )
        query_grads.append(query_grad[:rows])
        kv_own = ring_scatter(kv_term.reshape(count, rows, 2 * size))
        key_own = rotate(kv_own[:, :size], cosine[m], -sine[m])
        key_value_grads.append(jnp.concatenate([key_own, kv_own[:, size:]], axis=1).astype(BF16))

    query_grad = jnp.concatenate(query_grads, axis=0)
    kv_grad = jnp.concatenate(key_value_grads, axis=0)
    attended = jnp.concatenate([entry[3][:rows] for entry in saved], axis=0)
    grad_out = scatter_everywhere(
        contract_rows(jnp.concatenate(branch_grads, axis=0), attended, BF16)
    ).T
    grad_query = scatter_everywhere(contract_rows(normed, query_grad, BF16))

    attn_in_grad = contract_last(query_grad, query_full) + contract_last(kv_grad, w_kv)
    norm_back = jax.vjp(rms_scale, inputs, gain_first)[1]
    input_part, gain_one = norm_back(attn_in_grad.reshape(micros, rows, width))
    grad_tokens = jnp.stack(middle_grads) + input_part

    gain_cols = jnp.stack([gain_one, sum(gain_two)], axis=1).astype(BF16)
    narrow_grad = scatter_everywhere(
        jnp.concatenate(
            [contract_rows(normed, kv_grad, BF16), jnp.pad(gain_cols, ((0, 0), (0, 126)))], axis=1
        )
    )
    return (
        output[:, None],
        grad_tokens[:, None],
        narrow_grad[:, 2 * size],
        grad_query,
        narrow_grad[:, :size],
        narrow_grad[:, size : 2 * size],
        grad_out,
        narrow_grad[:, 2 * size + 1],
        grad_gate,
        grad_up,
        grad_down,
    )


def solution(mesh):
    rows = P(None, "wt", "ctx", None)
    everywhere = P(("ctx", "wt"))
    tall = P(("ctx", "wt"), None)
    wide = P(None, ("ctx", "wt"))
    square = P("ctx", "wt")
    return jax.shard_map(
        local,
        mesh=mesh,
        in_specs=(
            rows, P(None, "wt", "ctx"), rows, everywhere, tall, tall, tall, wide, everywhere,
            square, square, P("wt", "ctx"),
        ),
        out_specs=(
            rows, rows, everywhere, tall, tall, tall, wide, everywhere, square, square,
            P("wt", "ctx"),
        ),
        check_vma=False,
    )
```

```python
import functools
import math

import jax
import jax.numpy as jnp
from jax import lax
from jax.experimental import pallas as pl
from jax.experimental.pallas import tpu as pltpu
from jax.sharding import PartitionSpec as P

WINDOW = 2048
EPSILON = 1e-06
NEGATIVE = -1e30
LOG2E = math.log2(math.e)
LN2 = math.log(2.0)
F32 = jnp.float32
BF16 = jnp.bfloat16
SHORT = pl.CostEstimate(flops=1024, bytes_accessed=1024, transcendentals=0)


def rms_scale(values, gain):
    return values * lax.rsqrt(jnp.mean(values * values, axis=-1, keepdims=True) + EPSILON) * gain


def dot(left, right, out=F32):
    return jnp.dot(left, right, preferred_element_type=out)


def contract_rows(left, right, out=F32):
    return lax.dot_general(left, right, (((0,), (0,)), ((), ())), preferred_element_type=out)


def contract_last(left, right, out=F32):
    return lax.dot_general(left, right, (((1,), (1,)), ((), ())), preferred_element_type=out)


class Plan:
    def __init__(self):
        self.now = ()

    def hold(self, value):
        if not self.now:
            return value
        return lax.optimization_barrier((value,) + self.now)[0]

    def run(self, function, first, *rest):
        out = function(self.hold(first), *rest)
        self.now = tuple(jax.tree.leaves(out))
        return out

    def start(self, generator):
        return Transfer(self, generator)

    def step(self, *transfers):
        for transfer in transfers:
            transfer.step()


class Transfer:
    def __init__(self, plan, generator):
        self.plan, self.generator = plan, generator
        self.ended, self.value, self.passed = False, None, []
        self.launch(None)

    def launch(self, arrived):
        try:
            wanted = self.generator.send(arrived)
            while not isinstance(wanted, list):
                self.passed.append(wanted)
                wanted = next(self.generator)
        except StopIteration as stop:
            self.ended, self.value = True, stop.value
            return
        held = [self.plan.hold(operand) for operand, _, _ in wanted]
        self.flying = [
            lax.ppermute(operand, axis, pairs) for operand, (_, axis, pairs) in zip(held, wanted)
        ]
        self.plan.now = self.plan.now + tuple(operand for operand, _, _ in wanted)

    def step(self):
        if not self.ended:
            arrived = self.flying
            self.plan.now = self.plan.now + tuple(arrived)
            self.launch(arrived)

    def end(self):
        while not self.ended:
            self.step()
        return self.value


class Whole:
    def __init__(self, plan, function, operand):
        self.plan, self.value = plan, function(plan.hold(operand))

    def end(self):
        self.plan.now = self.plan.now + (self.value,)
        return self.value


def ctx_gather(block):
    return lax.all_gather(block, "ctx", axis=0, tiled=True)


def ctx_scatter(terms):
    return lax.psum_scatter(terms, "ctx", scatter_dimension=0, tiled=True)


def ring_order(count):
    return list(range(0, count, 2)) + [i for i in range(count - 1, 0, -1) if i % 2]


def ring(block, shift):
    count = lax.axis_size("ctx")
    order = ring_order(count)
    return block, "ctx", [(order[i], order[(i + shift) % count]) for i in range(count)]


def wt_swap(block, bit):
    return block, "wt", [(i, i ^ bit) for i in range(lax.axis_size("wt"))]


def core_swap(block):
    return wt_swap(block, 1)


def x_swap(block):
    return wt_swap(block, 2)


def ring_index(offset):
    count = lax.axis_size("ctx")
    here = lax.axis_index("ctx")
    place = jnp.where(here % 2 == 0, here // 2, count - 1 - here // 2)
    place = (place + offset + count) % count
    return jnp.where(place < count // 2, 2 * place, 2 * (count - 1 - place) + 1)


def half_rows(rows):
    return rows // 2 // 16 * 16 if rows >= 32 else rows // 2


def ring_blocks(block):
    half = lax.axis_size("ctx") // 2
    cut = half_rows(block.shape[0])
    ahead = behind = block
    for step in range(1, half):
        ahead, behind = yield [ring(ahead, 1), ring(behind, -1)], None
        yield None, [(-step, 0, ahead), (step, 0, behind)]
    low, high = yield [ring(ahead[:cut], 1), ring(behind[cut:], -1)], None
    yield None, [(half, 0, low), (half, cut, high)]


def put(found, piece, offset, row):
    start = (ring_index(offset), row) + (0,) * (piece.ndim - 1)
    return lax.dynamic_update_slice(found, piece[None], start)


def begin_kernel(place, block_ref, out_ref):
    del place
    out_ref[0] = block_ref[...]


def begin(block, count):
    shape = block.shape
    return pl.pallas_call(
        begin_kernel,
        out_shape=jax.ShapeDtypeStruct((count,) + shape, block.dtype),
        grid_spec=pltpu.PrefetchScalarGridSpec(
            num_scalar_prefetch=1,
            grid=(1,),
            in_specs=[pl.BlockSpec(shape, lambda i, place: (0, 0))],
            out_specs=pl.BlockSpec((1,) + shape, lambda i, place: (place[0], 0, 0)),
        ),
        cost_estimate=pl.CostEstimate(
            flops=0, bytes_accessed=4 * math.prod(shape), transcendentals=0
        ),
    )(lax.axis_index("ctx").reshape(1), block)


def ring_gather(block):
    found = begin(block, lax.axis_size("ctx"))
    blocks = ring_blocks(block)
    wanted, _ = next(blocks)
    while wanted is not None:
        arrived = yield wanted
        _, pieces = blocks.send(arrived)
        for offset, row, piece in pieces:
            found = put(found, piece, offset, row)
        wanted, _ = next(blocks, (None, None))
    return found


def ring_scatter(terms):
    half = terms.shape[0] // 2
    cut = half_rows(terms.shape[1])

    def own(offset):
        return lax.dynamic_index_in_dim(terms, ring_index(offset), 0, keepdims=False)

    far = own(half)
    ahead, behind = yield [ring(far[:cut], 1), ring(far[cut:], -1)]
    if half == 1:
        return own(0).astype(F32) + jnp.concatenate([ahead, behind], axis=0).astype(F32)
    for step in range(half - 1, 0, -1):
        up, down = own(step), own(-step)
        if step == half - 1:
            up = jnp.concatenate([add(up[:cut], ahead), up[cut:]], axis=0)
            down = jnp.concatenate([down[:cut], add(down[cut:], behind)], axis=0)
        else:
            up, down = add(up, ahead), add(down, behind)
        ahead, behind = yield [ring(up, 1), ring(down, -1)]
    return own(0).astype(F32) + ahead.astype(F32) + behind.astype(F32)


def add(first, second):
    return (first.astype(F32) + second.astype(F32)).astype(BF16)


def gather_everywhere(block):
    here = lax.axis_index("wt")
    width = block.shape[1]
    mine = begin(block, lax.axis_size("ctx"))
    far = None
    blocks = ring_blocks(block)
    crossing = [(0, 0, block)]
    wanted, _ = next(blocks)
    while wanted is not None or crossing:
        turns = wanted or []
        arrived = yield turns + [x_swap(piece) for _, _, piece in crossing]
        for (offset, row, _), piece in zip(crossing, arrived[len(turns) :]):
            far = begin(piece, mine.shape[0]) if far is None else put(far, piece, offset, row)
        crossing = []
        if wanted is not None:
            _, crossing = blocks.send(arrived[: len(turns)])
            for offset, row, piece in crossing:
                mine = put(mine, piece, offset, row)
            wanted, _ = next(blocks, (None, None))
    near, last = yield [core_swap(mine), core_swap(far)]
    return interleave(here, mine, near, far, last).reshape(-1, width)


def interleave_kernel(here, *refs):
    *pieces, out_ref = refs
    for bit, piece in enumerate(pieces):
        out_ref[0, here[0] ^ bit] = piece[0]


def interleave(here, *pieces):
    count, rows, width = pieces[0].shape
    return pl.pallas_call(
        interleave_kernel,
        out_shape=jax.ShapeDtypeStruct((count, 4, rows, width), pieces[0].dtype),
        grid_spec=pltpu.PrefetchScalarGridSpec(
            num_scalar_prefetch=1,
            grid=(count,),
            in_specs=[pl.BlockSpec((1, rows, width), lambda i, here: (i, 0, 0))] * 4,
            out_specs=pl.BlockSpec((1, 4, rows, width), lambda i, here: (i, 0, 0, 0)),
        ),
        cost_estimate=SHORT,
    )(here.reshape(1), *pieces)


def scatter_everywhere(terms):
    here = lax.axis_index("wt")
    count = lax.axis_size("ctx")
    rows = terms.shape[0] // (4 * count)
    split = terms.reshape(count, 2, 2, rows, terms.shape[1])
    x_here, core_here = here // 2, here % 2
    sent = lax.dynamic_index_in_dim(split, 1 - core_here, 2, keepdims=False)
    (came,) = yield [core_swap(sent)]
    both = add(lax.dynamic_index_in_dim(split, core_here, 2, keepdims=False), came)
    sent = lax.dynamic_index_in_dim(both, 1 - x_here, 1, keepdims=False)
    (came,) = yield [x_swap(sent)]
    kept = add(lax.dynamic_index_in_dim(both, x_here, 1, keepdims=False), came)
    return (yield from ring_scatter(kept))


def once(permute):
    (came,) = yield [permute]
    return came


def rows_there(block):
    (far,) = yield [x_swap(block)]
    (last,) = yield [core_swap(far)]
    return [far, last]


def scatter_here(terms):
    rows = terms.shape[0] // 2
    (near,) = yield [core_swap(terms[rows:])]
    return terms[:rows].astype(F32) + near.astype(F32)


def scatter_there(terms, parts):
    rows = terms.shape[0] // 2
    (last,) = yield [core_swap(terms[rows:])]
    far = add(terms[:rows], last)
    came = []
    for part in jnp.split(far, parts):
        came += yield [x_swap(part)]
        yield came[-1]
    return jnp.concatenate(came, axis=0)


def rotate(values, cosine, sine):
    half = values.shape[-1] // 2
    first, second = values[:, :half], values[:, half:]
    return jnp.concatenate(
        [first * cosine - second * sine, second * cosine + first * sine], axis=-1
    )


def visible(start, keys, low, high):
    index = start + lax.broadcasted_iota(jnp.int32, (keys, low.shape[1]), 0)
    return (index >= low) & (index <= high)


def key_parts(keys):
    return [slice(0, keys)]


def attend_kernel(
    spans, q_ref, kv_ref, low_ref, high_ref, cos_ref, sin_ref,
    out_ref, qrot_ref, lse_ref, vt_ref, *, heads, size, keys,
):
    rows = q_ref.shape[0]
    scale = size ** -0.5 * LOG2E

    @pl.when(pl.program_id(0) == 0)
    def _():
        for block in range(kv_ref.shape[0]):
            vt_ref[block] = kv_ref[block, :, size:].T

    turned = []
    for head in range(heads):
        part = rotate(q_ref[:, head * size : (head + 1) * size], cos_ref[...], sin_ref[...])
        part = (part * scale).astype(BF16)
        qrot_ref[:, head * size : (head + 1) * size] = part
        turned.append(part.T)
    qt = jnp.concatenate(turned, axis=1)
    low, high = low_ref[...], high_ref[...]
    parts = key_parts(keys)

    def step(block, carry, masked):
        top, total, acc = carry
        scores = []
        for part in parts:
            piece = dot(kv_ref[block, part, :size], qt)
            if masked:
                seen = visible(block * keys + part.start, part.stop - part.start, low, high)
                piece = jnp.where(seen, piece, NEGATIVE)
            scores.append(piece)
        new_top = top
        for piece in scores:
            new_top = jnp.maximum(new_top, jnp.max(piece, axis=0, keepdims=True))
        fade = jnp.exp2(top - new_top)
        total = total * fade
        acc = acc * fade
        for part, piece in zip(parts, scores):
            probs = jnp.exp2(piece - new_top)
            total = total + jnp.sum(probs, axis=0, keepdims=True)
            acc = acc + dot(vt_ref[block, :, part], probs.astype(BF16))
        return new_top, total, acc

    carry = (
        jnp.full((1, heads * rows), NEGATIVE, F32),
        jnp.zeros((1, heads * rows), F32),
        jnp.zeros((size, heads * rows), F32),
    )
    carry = lax.fori_loop(spans[0], spans[1], functools.partial(step, masked=True), carry)
    carry = lax.fori_loop(spans[2], spans[3], functools.partial(step, masked=False), carry)
    carry = lax.fori_loop(spans[4], spans[5], functools.partial(step, masked=True), carry)
    top, total, acc = carry
    acc = acc * (1.0 / total)
    lse_ref[0] = top + jnp.log2(total)
    for head in range(heads):
        out_ref[:, head * size : (head + 1) * size] = (
            acc[:, head * rows : (head + 1) * rows].astype(BF16).T
        )


def attend_back_kernel(
    spans, q_ref, kv_ref, low_ref, high_ref, cos_ref, sin_ref, out_ref, grad_ref, lse_ref,
    dq_ref, dkv_ref, kt_ref, dk_ref, dv_ref, *, heads, size, keys,
):
    rows = q_ref.shape[0]

    @pl.when(pl.program_id(0) == 0)
    def _():
        for block in range(kv_ref.shape[0]):
            kt_ref[block] = kv_ref[block, :, :size].T
        dk_ref[...] = jnp.zeros_like(dk_ref)
        dv_ref[...] = jnp.zeros_like(dv_ref)

    parts = [slice(head * size, (head + 1) * size) for head in range(heads)]
    q = jnp.concatenate([q_ref[:, part] for part in parts], axis=0)
    grad = jnp.concatenate([grad_ref[:, part] for part in parts], axis=0)
    out_t = jnp.concatenate([out_ref[:, part].T for part in parts], axis=1)
    qt, grad_t = q.T, grad.T
    delta = jnp.sum(grad_t.astype(F32) * out_t.astype(F32), axis=0, keepdims=True)
    low, high, lse = low_ref[...], high_ref[...], lse_ref[0]

    def step(block, dq, masked):
        for part in key_parts(keys):
            scores = dot(kv_ref[block, part, :size], qt)
            if masked:
                seen = visible(block * keys + part.start, part.stop - part.start, low, high)
                scores = jnp.where(seen, scores, NEGATIVE)
            probs = jnp.exp2(scores - lse)
            probs_grad = dot(kv_ref[block, part, size:], grad_t)
            score_grad = (probs * (probs_grad - delta)).astype(BF16)
            dv_ref[block, part] += dot(probs.astype(BF16), grad)
            dk_ref[block, part] += dot(score_grad, q)
            dq = dq + dot(kt_ref[block, :, part], score_grad)
        return dq

    dq = jnp.zeros((size, heads * rows), F32)
    dq = lax.fori_loop(spans[0], spans[1], functools.partial(step, masked=True), dq)
    dq = lax.fori_loop(spans[2], spans[3], functools.partial(step, masked=False), dq)
    dq = lax.fori_loop(spans[4], spans[5], functools.partial(step, masked=True), dq)
    for head, part in enumerate(parts):
        turned = rotate(dq[:, head * rows : (head + 1) * rows].T, cos_ref[...], -sin_ref[...])
        dq_ref[:, part] = (turned * size ** -0.5).astype(BF16)

    @pl.when(pl.program_id(0) == pl.num_programs(0) - 1)
    def _():
        for block in range(dkv_ref.shape[0]):
            dkv_ref[block, :, :size] = (dk_ref[block] * LN2).astype(BF16)
            dkv_ref[block, :, size:] = dv_ref[block].astype(BF16)


def attention_calls(rows, width, size, count, keys, micro):
    heads = 2 if (width // size) % 2 == 0 else 1
    groups = width // size // heads
    span = heads * size
    head_block = pl.BlockSpec((rows, span), lambda g, s: (0, g))

    def whole(*shape):
        return pl.BlockSpec(shape, lambda g, s: (0,) * len(shape))

    lse_block = pl.BlockSpec((1, 1, heads * rows), lambda g, s: (g, 0, 0))
    shared = [
        head_block,
        pl.BlockSpec((count, keys, 2 * size), lambda g, s: (0, micro, 0)),
        whole(1, heads * rows), whole(1, heads * rows),
        whole(rows, size // 2), whole(rows, size // 2),
    ]
    lse_shape = jax.ShapeDtypeStruct((groups, 1, heads * rows), F32)
    row_shape = jax.ShapeDtypeStruct((rows, width), BF16)
    params = pltpu.CompilerParams(vmem_limit_bytes=48 * 2**20)
    work = rows * width * min(count * keys, WINDOW) * 2
    sizes = dict(heads=heads, size=size, keys=keys)
    forward = pl.pallas_call(
        functools.partial(attend_kernel, **sizes),
        out_shape=(row_shape, row_shape, lse_shape),
        grid_spec=pltpu.PrefetchScalarGridSpec(
            num_scalar_prefetch=1, grid=(groups,), in_specs=shared,
            out_specs=(head_block, head_block, lse_block),
            scratch_shapes=[pltpu.VMEM((count, size, keys), BF16)],
        ),
        compiler_params=params,
        cost_estimate=SHORT,
    )
    backward = pl.pallas_call(
        functools.partial(attend_back_kernel, **sizes),
        out_shape=(row_shape, jax.ShapeDtypeStruct((count, keys, 2 * size), BF16)),
        grid_spec=pltpu.PrefetchScalarGridSpec(
            num_scalar_prefetch=1, grid=(groups,),
            in_specs=shared + [head_block, head_block, lse_block],
            out_specs=(head_block, whole(count, keys, 2 * size)),
            scratch_shapes=[
                pltpu.VMEM((count, size, keys), BF16),
                pltpu.VMEM((count, keys, size), F32),
                pltpu.VMEM((count, keys, size), F32),
            ],
        ),
        compiler_params=params,
        cost_estimate=SHORT,
    )
    return forward, backward, heads


def pad_rows(array, rows):
    return jnp.pad(array, ((0, rows - array.shape[0]), (0, 0)))


def weight_kernel(a_here, a_there, b_here, b_there, out_ref):
    out_ref[...] = (
        contract_rows(a_here[...], b_here[...]) + contract_rows(a_there[...], b_there[...])
    ).astype(BF16)


def weight_grad(left, right):
    rows, width = left[0].shape
    cols = right[0].shape[1]
    tile = 256 if width % 256 == 0 else 128

    def column(array):
        return pl.BlockSpec((rows, tile), lambda i: (0, i))

    def fixed(array):
        return pl.BlockSpec(array.shape, lambda i: (0, 0), pipeline_mode=pl.Buffered(1))

    return pl.pallas_call(
        weight_kernel,
        out_shape=jax.ShapeDtypeStruct((width, cols), BF16),
        grid=(width // tile,),
        in_specs=[column(a) for a in left] + [fixed(a) for a in right],
        out_specs=pl.BlockSpec((tile, cols), lambda i: (i, 0)),
        compiler_params=pltpu.CompilerParams(vmem_limit_bytes=48 * 2**20),
        cost_estimate=pl.CostEstimate(
            flops=4 * rows * width * cols,
            bytes_accessed=4 * rows * (width + cols) + 2 * width * cols,
            transcendentals=0,
        ),
    )(*left, *right)


def local(
    tokens, segment_ids, cotangent, gain_attn, w_query, w_key, w_value, w_out, gain_mlp,
    w_gate, w_up, w_down,
):
    micros, _, rows, width = tokens.shape
    size = w_key.shape[1]
    query_width = w_query.shape[1]
    hidden_cols = w_gate.shape[1]
    count = lax.axis_size("ctx")
    first = lax.axis_index("ctx") * rows
    padded = -(-rows // 128) * 128
    calls = [
        attention_calls(padded, query_width, size, count, rows, m) for m in range(micros)
    ]
    heads = calls[0][2]
    plan = Plan()

    ids = segment_ids[:, 0]
    slots = w_key.shape[0]
    id_cols = -(-micros * rows // slots)
    id_flat = jnp.pad(ids.reshape(-1), (0, id_cols * slots - micros * rows)).astype(BF16)
    beside = jnp.concatenate(
        [jnp.stack([gain_attn, gain_mlp], axis=1), id_flat.reshape(slots, id_cols)], axis=1
    )
    beside = jnp.pad(beside, ((0, 0), (0, -beside.shape[1] % 128)))
    everyone = ("ctx", "wt")
    narrow_in = Whole(
        plan, lambda block: lax.all_gather(block, everyone, axis=0, tiled=True),
        jnp.concatenate([w_key, w_value, beside], axis=1),
    )
    query_in = plan.start(gather_everywhere(w_query))
    plan.step(query_in)
    plan.step(query_in)
    narrow_full = narrow_in.end()
    narrow_ring = lax.dynamic_index_in_dim(
        narrow_full.reshape(count, 4, slots, -1), lax.axis_index("wt"), 1, keepdims=False
    )
    w_kv = narrow_full[:, : 2 * size]
    gain_first = narrow_full[:, 2 * size].astype(F32)
    gain_second = narrow_full[:, 2 * size + 1].astype(F32)
    ids_all = narrow_ring[:, :, 2 * size + 2 : 2 * size + 2 + id_cols].reshape(count, -1)
    ids_all = ids_all[:, : micros * rows].reshape(count, micros, rows)
    ids_all = ids_all.transpose(1, 0, 2).reshape(micros, count * rows).astype(jnp.int32)

    index = first + jnp.arange(rows, dtype=jnp.int32)
    half = size // 2

    def tables(index):
        freqs = 10000.0 ** (-jnp.arange(half, dtype=F32) / half)
        angles = index.astype(F32)[:, None] * freqs
        return jnp.cos(angles), jnp.sin(angles)

    cosine, sine = tables(index)
    begins = jnp.sum(
        (ids_all[:, None, :] < ids[:, :, None]).astype(jnp.int32), axis=-1, dtype=jnp.int32
    )
    lowest = jnp.maximum(begins, index[None] - (WINDOW - 1))

    def project_kv(rows_in, gain, weights, cosine, sine):
        normed = rms_scale(rows_in[:, 0].astype(F32), gain).astype(BF16)
        normed = normed.reshape(micros * rows, width)
        both = dot(normed, weights)
        keys = both[:, :size].astype(BF16).astype(F32)
        twice = [jnp.concatenate([t] * micros, axis=0) for t in (cosine, sine)]
        return normed, jnp.concatenate([rotate(keys, *twice), both[:, size:]], axis=1).astype(BF16)

    normed, turned = plan.run(project_kv, tokens, gain_first, w_kv, cosine, sine)
    kv_in = Whole(plan, ctx_gather, turned)
    plan.step(query_in)
    plan.step(query_in)
    out_in = plan.start(gather_everywhere(plan.hold(w_out).T))
    plan.step(query_in)
    plan.step(out_in)
    query_full = query_in.end()
    cot = plan.hold(cotangent).reshape(micros * rows, width)
    cot_near, cot_far = plan.start(once(core_swap(cot))), plan.start(rows_there(cot))
    queries = plan.run(lambda a, b: dot(a, b).reshape(micros, rows, -1), normed, query_full)
    plan.step(out_in)
    kv_all = kv_in.end().reshape(count, micros * rows, 2 * size)
    gate_in = Whole(plan, ctx_gather, w_gate)
    plan.step(out_in)

    saved = []
    for m in range(micros):
        full_from = (jnp.max(lowest[m]) + rows - 1) // rows
        full_to = (first + 1) // rows
        last = (first + rows - 1) // rows + 1
        spans = jnp.stack([
            jnp.min(lowest[m]) // rows, jnp.minimum(full_from, last),
            full_from, full_to,
            jnp.maximum(full_from, full_to), last,
        ]).astype(jnp.int32)

        def lanes(values):
            return jnp.tile(jnp.pad(values, (0, padded - rows))[None], (1, heads))

        shared = (
            kv_all, lanes(lowest[m]), lanes(index),
            pad_rows(cosine, padded), pad_rows(sine, padded),
        )
        attended, query_rot, lse = plan.run(
            lambda q, s, *rest: calls[m][0](s, q, *rest),
            pad_rows(queries[m], padded), spans, *shared,
        )
        saved.append((spans, query_rot, shared, attended, lse))
        plan.step(out_in)

    attended = jnp.concatenate([entry[3][:rows] for entry in saved], axis=0)
    plan.step(cot_near, cot_far)
    out_full = out_in.end()

    def join(attended, tokens, weights, gain):
        middle = tokens.reshape(micros * rows, width).astype(F32) + contract_last(attended, weights)
        return middle, rms_scale(middle, gain).astype(BF16)

    middle, low = plan.run(join, attended, tokens, out_full, gain_second)
    near_in, far_in = plan.start(once(core_swap(low))), plan.start(rows_there(low))

    cot_rows = [
        jnp.concatenate([cot, cot_near.end()], axis=0), jnp.concatenate(cot_far.end(), axis=0)
    ]
    gate_full = gate_in.end()
    up_in = Whole(plan, ctx_gather, w_up)
    normed_rows = [
        jnp.concatenate([low, near_in.end()], axis=0), jnp.concatenate(far_in.end(), axis=0)
    ]
    gate_rows = [plan.run(dot, rows_in, gate_full) for rows_in in normed_rows]
    up_full = up_in.end()
    down_in = Whole(plan, ctx_gather, w_down.T)

    def make_hidden(rows_in, weights, gate):
        up = dot(rows_in, weights)
        return up, (jax.nn.gelu(gate) * up).astype(BF16)

    up_rows, hidden = [], []
    for side in range(2):
        up, both = plan.run(make_hidden, normed_rows[side], up_full, gate_rows[side])
        up_rows.append(up)
        hidden.append(both)

    def weight_sum(left, right):
        terms = plan.run(lambda a, *rest: weight_grad((a, left[1]), right), left[0])
        return Whole(plan, ctx_scatter, terms)

    down_out = weight_sum(cot_rows, hidden)
    down_full = down_in.end()

    def both_halves(function, parts, between=None):
        there = plan.start(scatter_there(function(1), parts))
        if between is not None:
            between()
        here = plan.start(scatter_here(function(0)))
        plan.step(there)
        return here, there

    mlp_here, mlp_there = both_halves(
        lambda side: plan.run(lambda a, b: contract_last(a, b, BF16), hidden[side], down_full), 1
    )

    def hidden_back(cot, weights, gate, up):
        hidden_grad = dot(cot, weights)
        gelu_gate, gelu_back = jax.vjp(jax.nn.gelu, gate)
        gate_grad = gelu_back(hidden_grad * up)[0].astype(BF16)
        return gate_grad, (hidden_grad * gelu_gate).astype(BF16)

    gate_grad, up_grad = [None, None], [None, None]
    for side in range(2):
        gate_grad[side], up_grad[side] = plan.run(
            hidden_back, cot_rows[side], down_full, gate_rows[side], up_rows[side]
        )
    mlp_own = mlp_here.end()
    gate_out = weight_sum(normed_rows, gate_grad)
    mlp_came = mlp_there.end()

    def rows_back(side):
        part = plan.run(contract_last, gate_grad[side], gate_full)
        return plan.run(
            lambda a, b, c: (contract_last(a, b) + c).astype(BF16), up_grad[side], up_full, part
        )

    back_here, back_there = both_halves(rows_back, micros, down_out.end)
    up_terms = plan.run(
        lambda a, *rest: weight_grad((a, normed_rows[1]), up_grad), normed_rows[0]
    )
    up_out = plan.start(ring_scatter(up_terms.reshape(count, -1, hidden_cols)))

    middle_grads, branch_grads, attended_grads, gain_two = [], [], [], []
    query_grads, kv_out = [], []
    back_own = back_here.end()

    def join_back(came, own, middle, gain, cot):
        incoming = own + came.astype(F32)
        middle_part, gain_part = jax.vjp(rms_scale, middle, gain)[1](incoming)
        middle_grad = middle_part + cot.astype(F32)
        return middle_grad, middle_grad.astype(BF16), gain_part

    def before_attention(m):
        here = slice(m * rows, (m + 1) * rows)
        middle_grad, branch_grad, gain_part = plan.run(
            join_back, back_there.passed[m], back_own[here], middle[here], gain_second, cot[here]
        )
        middle_grads.append(middle_grad)
        branch_grads.append(branch_grad)
        gain_two.append(gain_part)
        attended_grads.append(plan.run(lambda a, b: dot(a, b, BF16), branch_grad, out_full))

    def through_attention(m):
        spans, query_rot, shared, attended, lse = saved[m]
        query_grad, kv_term = plan.run(
            lambda g, s, q, shared, out, lse: calls[m][1](s, q, *shared, out, g, lse),
            pad_rows(attended_grads[m], padded), spans, query_rot, shared, attended, lse,
        )
        query_grads.append(query_grad[:rows])
        kv_out.append(plan.start(ring_scatter(kv_term)))

    plan.step(back_there)
    plan.step(up_out)
    before_attention(0)
    through_attention(0)
    gate_out.end()
    plan.step(up_out)
    plan.step(back_there)
    before_attention(1)
    plan.step(kv_out[0])
    plan.step(up_out)
    out_out = plan.start(scatter_everywhere(
        plan.run(
            lambda a, b: contract_rows(a, b, BF16), jnp.concatenate(branch_grads, axis=0), attended
        )
    ))
    plan.step(kv_out[0])
    plan.step(out_out)
    through_attention(1)
    plan.step(kv_out[0])
    plan.step(up_out)
    query_grad = jnp.concatenate(query_grads, axis=0)
    query_out = plan.start(scatter_everywhere(
        plan.run(lambda a, b: contract_rows(a, b, BF16), normed, query_grad)
    ))
    plan.step(kv_out[0])
    plan.step(kv_out[1])
    plan.step(query_out)
    plan.step(out_out)
    part = plan.run(contract_last, query_grad, query_full)
    plan.step(kv_out[1])

    def finish_output(came, own, middle):
        return (middle + own + came.astype(F32)).reshape(micros, rows, width)

    output = plan.run(finish_output, mlp_came, mlp_own, middle)
    plan.step(kv_out[1])
    plan.step(out_out)
    kv_own = jnp.concatenate([t.end() for t in kv_out], axis=0)
    twice = [jnp.concatenate([t] * micros, axis=0) for t in (cosine, sine)]
    key_own = rotate(kv_own[:, :size], twice[0], -twice[1])
    kv_grad = jnp.concatenate([key_own, kv_own[:, size:]], axis=1).astype(BF16)

    def narrow_back(kv_grad, normed):
        return contract_rows(normed, kv_grad, BF16)

    def inputs_back(kv_grad, part, weights, tokens, gain, middle_grads):
        attn_in_grad = part + contract_last(kv_grad, weights)
        norm_back = jax.vjp(rms_scale, tokens[:, 0].astype(F32), gain)[1]
        input_part, gain_one = norm_back(attn_in_grad.reshape(micros, rows, width))
        return jnp.stack(middle_grads) + input_part, gain_one

    kv_terms = plan.run(narrow_back, kv_grad, normed)
    grad_tokens, gain_one = plan.run(
        inputs_back, kv_grad, part, w_kv, tokens, gain_first, middle_grads
    )
    gain_cols = jnp.stack([gain_one, sum(gain_two)], axis=1).astype(BF16)
    narrow_out = plan.start(scatter_everywhere(
        jnp.concatenate([kv_terms, jnp.pad(gain_cols, ((0, 0), (0, 126)))], axis=1)
    ))
    for _ in range(count):
        plan.step(narrow_out, out_out, query_out)
    narrow_grad = narrow_out.end()
    return (
        output[:, None],
        grad_tokens[:, None],
        narrow_grad[:, 2 * size],
        query_out.end(),
        narrow_grad[:, :size],
        narrow_grad[:, size : 2 * size],
        out_out.end().T,
        narrow_grad[:, 2 * size + 1],
        gate_out.value.astype(F32),
        up_out.end(),
        down_out.value.T.astype(F32),
    )


def solution(mesh):
    rows = P(None, "wt", "ctx", None)
    everywhere = P(("ctx", "wt"))
    tall = P(("ctx", "wt"), None)
    wide = P(None, ("ctx", "wt"))
    square = P("ctx", "wt")
    return jax.shard_map(
        local,
        mesh=mesh,
        in_specs=(
            rows, P(None, "wt", "ctx"), rows, everywhere, tall, tall, tall, wide, everywhere,
            square, square, P("wt", "ctx"),
        ),
        out_specs=(
            rows, rows, everywhere, tall, tall, tall, wide, everywhere, square, square,
            P("wt", "ctx"),
        ),
        check_vma=False,
    )
```

```python
import functools
import math

import jax
import jax.numpy as jnp
from jax import lax
from jax.experimental import pallas as pl
from jax.experimental.pallas import tpu as pltpu
from jax.sharding import PartitionSpec as P

WINDOW = 2048
EPSILON = 1e-06
NEGATIVE = -1e30
LOG2E = math.log2(math.e)
LN2 = math.log(2.0)
F32 = jnp.float32
BF16 = jnp.bfloat16


def rms_scale(values, gain):
    return values * lax.rsqrt(jnp.mean(values * values, axis=-1, keepdims=True) + EPSILON) * gain


def dot(left, right, out=F32):
    return jnp.dot(left, right, preferred_element_type=out)


def contract_rows(left, right, out=F32):
    return lax.dot_general(left, right, (((0,), (0,)), ((), ())), preferred_element_type=out)


def contract_last(left, right, out=F32):
    return lax.dot_general(left, right, (((1,), (1,)), ((), ())), preferred_element_type=out)


class Plan:
    def __init__(self):
        self.now = ()

    def hold(self, value):
        if not self.now:
            return value
        return lax.optimization_barrier((value,) + self.now)[0]

    def run(self, function, first, *rest):
        out = function(self.hold(first), *rest)
        self.now = tuple(jax.tree.leaves(out))
        return out

    def start(self, generator):
        return Transfer(self, generator)

    def step(self, *transfers):
        for transfer in transfers:
            transfer.step()


class Transfer:
    def __init__(self, plan, generator):
        self.plan, self.generator = plan, generator
        self.ended, self.value, self.passed = False, None, []
        self.launch(None)

    def launch(self, arrived):
        try:
            wanted = self.generator.send(arrived)
            while not isinstance(wanted, list):
                self.passed.append(wanted)
                wanted = next(self.generator)
        except StopIteration as stop:
            self.ended, self.value = True, stop.value
            return
        held = [self.plan.hold(operand) for operand, _, _ in wanted]
        self.flying = [
            lax.ppermute(operand, axis, pairs) for operand, (_, axis, pairs) in zip(held, wanted)
        ]
        self.plan.now = self.plan.now + tuple(operand for operand, _, _ in wanted)

    def step(self):
        if not self.ended:
            arrived = self.flying
            self.plan.now = self.plan.now + tuple(arrived)
            self.launch(arrived)

    def end(self):
        while not self.ended:
            self.step()
        return self.value


class Whole:
    def __init__(self, plan, function, operand):
        self.plan, self.value = plan, function(plan.hold(operand))

    def end(self):
        self.plan.now = self.plan.now + (self.value,)
        return self.value


def ctx_gather(block):
    return lax.all_gather(block, "ctx", axis=0, tiled=True)


def ctx_scatter(terms):
    return lax.psum_scatter(terms, "ctx", scatter_dimension=0, tiled=True)


def ring_order(count):
    return list(range(0, count, 2)) + [i for i in range(count - 1, 0, -1) if i % 2]


def ring(block, shift):
    count = lax.axis_size("ctx")
    order = ring_order(count)
    return block, "ctx", [(order[i], order[(i + shift) % count]) for i in range(count)]


def wt_swap(block, bit):
    return block, "wt", [(i, i ^ bit) for i in range(lax.axis_size("wt"))]


def core_swap(block):
    return wt_swap(block, 1)


def x_swap(block):
    return wt_swap(block, 2)


def ring_index(offset):
    count = lax.axis_size("ctx")
    here = lax.axis_index("ctx")
    place = jnp.where(here % 2 == 0, here // 2, count - 1 - here // 2)
    place = (place + offset + count) % count
    return jnp.where(place < count // 2, 2 * place, 2 * (count - 1 - place) + 1)


def half_rows(rows):
    return rows // 2 // 16 * 16 if rows >= 32 else rows // 2


def ring_blocks(block):
    half = lax.axis_size("ctx") // 2
    cut = half_rows(block.shape[0])
    ahead = behind = block
    for step in range(1, half):
        ahead, behind = yield [ring(ahead, 1), ring(behind, -1)], None
        yield None, [(-step, 0, ahead), (step, 0, behind)]
    low, high = yield [ring(ahead[:cut], 1), ring(behind[cut:], -1)], None
    yield None, [(half, 0, low), (half, cut, high)]


def put(found, piece, offset, row):
    start = (ring_index(offset), row) + (0,) * (piece.ndim - 1)
    return lax.dynamic_update_slice(found, piece[None], start)


def begin_kernel(place, block_ref, out_ref):
    del place
    out_ref[0] = block_ref[...]


def begin(block, count):
    shape = block.shape
    return pl.pallas_call(
        begin_kernel,
        out_shape=jax.ShapeDtypeStruct((count,) + shape, block.dtype),
        grid_spec=pltpu.PrefetchScalarGridSpec(
            num_scalar_prefetch=1,
            grid=(1,),
            in_specs=[pl.BlockSpec(shape, lambda i, place: (0, 0))],
            out_specs=pl.BlockSpec((1,) + shape, lambda i, place: (place[0], 0, 0)),
        ),
        cost_estimate=pl.CostEstimate(
            flops=0, bytes_accessed=4 * math.prod(shape), transcendentals=0
        ),
    )(lax.axis_index("ctx").reshape(1), block)


def ring_gather(block):
    found = begin(block, lax.axis_size("ctx"))
    blocks = ring_blocks(block)
    wanted, _ = next(blocks)
    while wanted is not None:
        arrived = yield wanted
        _, pieces = blocks.send(arrived)
        for offset, row, piece in pieces:
            found = put(found, piece, offset, row)
        wanted, _ = next(blocks, (None, None))
    return found


def ring_scatter(terms):
    half = terms.shape[0] // 2
    cut = half_rows(terms.shape[1])

    def own(offset):
        return lax.dynamic_index_in_dim(terms, ring_index(offset), 0, keepdims=False)

    far = own(half)
    ahead, behind = yield [ring(far[:cut], 1), ring(far[cut:], -1)]
    if half == 1:
        return own(0).astype(F32) + jnp.concatenate([ahead, behind], axis=0).astype(F32)
    for step in range(half - 1, 0, -1):
        up, down = own(step), own(-step)
        if step == half - 1:
            up = jnp.concatenate([add(up[:cut], ahead), up[cut:]], axis=0)
            down = jnp.concatenate([down[:cut], add(down[cut:], behind)], axis=0)
        else:
            up, down = add(up, ahead), add(down, behind)
        ahead, behind = yield [ring(up, 1), ring(down, -1)]
    return own(0).astype(F32) + ahead.astype(F32) + behind.astype(F32)


def add(first, second):
    return (first.astype(F32) + second.astype(F32)).astype(BF16)


def gather_everywhere(block):
    here = lax.axis_index("wt")
    width = block.shape[1]
    mine = begin(block, lax.axis_size("ctx"))
    far = None
    blocks = ring_blocks(block)
    crossing = [(0, 0, block)]
    wanted, _ = next(blocks)
    while wanted is not None or crossing:
        turns = wanted or []
        arrived = yield turns + [x_swap(piece) for _, _, piece in crossing]
        for (offset, row, _), piece in zip(crossing, arrived[len(turns) :]):
            far = begin(piece, mine.shape[0]) if far is None else put(far, piece, offset, row)
        crossing = []
        if wanted is not None:
            _, crossing = blocks.send(arrived[: len(turns)])
            for offset, row, piece in crossing:
                mine = put(mine, piece, offset, row)
            wanted, _ = next(blocks, (None, None))
    near, last = yield [core_swap(mine), core_swap(far)]
    return interleave(here, mine, near, far, last).reshape(-1, width), mine


def interleave_kernel(here, *refs):
    *pieces, out_ref = refs
    for bit, piece in enumerate(pieces):
        out_ref[0, here[0] ^ bit] = piece[0]


def interleave(here, *pieces):
    count, rows, width = pieces[0].shape
    return pl.pallas_call(
        interleave_kernel,
        out_shape=jax.ShapeDtypeStruct((count, 4, rows, width), pieces[0].dtype),
        grid_spec=pltpu.PrefetchScalarGridSpec(
            num_scalar_prefetch=1,
            grid=(count,),
            in_specs=[pl.BlockSpec((1, rows, width), lambda i, here: (i, 0, 0))] * 4,
            out_specs=pl.BlockSpec((1, 4, rows, width), lambda i, here: (i, 0, 0, 0)),
        ),
        cost_estimate=pl.CostEstimate(
            flops=0, bytes_accessed=16 * count * rows * width, transcendentals=0
        ),
    )(here.reshape(1), *pieces)


def scatter_everywhere(terms):
    here = lax.axis_index("wt")
    count = lax.axis_size("ctx")
    rows = terms.shape[0] // (4 * count)
    split = terms.reshape(count, 2, 2, rows, terms.shape[1])
    x_here, core_here = here // 2, here % 2
    sent = lax.dynamic_index_in_dim(split, 1 - core_here, 2, keepdims=False)
    (came,) = yield [core_swap(sent)]
    both = add(lax.dynamic_index_in_dim(split, core_here, 2, keepdims=False), came)
    sent = lax.dynamic_index_in_dim(both, 1 - x_here, 1, keepdims=False)
    (came,) = yield [x_swap(sent)]
    kept = add(lax.dynamic_index_in_dim(both, x_here, 1, keepdims=False), came)
    return (yield from ring_scatter(kept))


def once(permute):
    (came,) = yield [permute]
    return came


def rows_there(block):
    (far,) = yield [x_swap(block)]
    (last,) = yield [core_swap(far)]
    return [far, last]


def scatter_here(terms):
    rows = terms.shape[0] // 2
    (near,) = yield [core_swap(terms[rows:])]
    return terms[:rows].astype(F32) + near.astype(F32)


def scatter_there(terms, parts):
    rows = terms.shape[0] // 2
    (last,) = yield [core_swap(terms[rows:])]
    far = add(terms[:rows], last)
    came = []
    for part in jnp.split(far, parts):
        came += yield [x_swap(part)]
        yield came[-1]
    return jnp.concatenate(came, axis=0)


def rotate(values, cosine, sine):
    half = values.shape[-1] // 2
    first, second = values[:, :half], values[:, half:]
    return jnp.concatenate(
        [first * cosine - second * sine, second * cosine + first * sine], axis=-1
    )


def visible(start, keys, low, high):
    index = start + lax.broadcasted_iota(jnp.int32, (keys, low.shape[1]), 0)
    return (index >= low) & (index <= high)


def attend_kernel(
    spans, q_ref, kv_ref, low_ref, high_ref, cos_ref, sin_ref,
    out_ref, qrot_ref, lse_ref, vt_ref, *, heads, size, keys,
):
    rows = q_ref.shape[0]
    scale = size ** -0.5 * LOG2E

    @pl.when(pl.program_id(0) == 0)
    def _():
        for block in range(kv_ref.shape[0]):
            vt_ref[block] = kv_ref[block, :, size:].T

    turned = []
    for head in range(heads):
        part = rotate(q_ref[:, head * size : (head + 1) * size], cos_ref[...], sin_ref[...])
        part = (part * scale).astype(BF16)
        qrot_ref[:, head * size : (head + 1) * size] = part
        turned.append(part.T)
    qt = jnp.concatenate(turned, axis=1)
    low, high = low_ref[...], high_ref[...]

    def step(block, carry, masked):
        top, total, acc = carry
        scores = dot(kv_ref[block, :, :size], qt)
        if masked:
            scores = jnp.where(visible(block * keys, keys, low, high), scores, NEGATIVE)
        new_top = jnp.maximum(top, jnp.max(scores, axis=0, keepdims=True))
        probs = jnp.exp2(scores - new_top)
        fade = jnp.exp2(top - new_top)
        total = total * fade + jnp.sum(probs, axis=0, keepdims=True)
        acc = acc * fade + dot(vt_ref[block], probs.astype(BF16))
        return new_top, total, acc

    carry = (
        jnp.full((1, heads * rows), NEGATIVE, F32),
        jnp.zeros((1, heads * rows), F32),
        jnp.zeros((size, heads * rows), F32),
    )
    carry = lax.fori_loop(spans[0], spans[1], functools.partial(step, masked=True), carry)
    carry = lax.fori_loop(spans[2], spans[3], functools.partial(step, masked=False), carry)
    carry = lax.fori_loop(spans[4], spans[5], functools.partial(step, masked=True), carry)
    top, total, acc = carry
    acc = acc * (1.0 / total)
    lse_ref[0] = top + jnp.log2(total)
    for head in range(heads):
        out_ref[:, head * size : (head + 1) * size] = (
            acc[:, head * rows : (head + 1) * rows].astype(BF16).T
        )


def attend_back_kernel(
    spans, q_ref, kv_ref, low_ref, high_ref, cos_ref, sin_ref, out_ref, grad_ref, lse_ref,
    dq_ref, dkv_ref, kt_ref, dk_ref, dv_ref, *, heads, size, keys,
):
    rows = q_ref.shape[0]

    @pl.when(pl.program_id(0) == 0)
    def _():
        for block in range(kv_ref.shape[0]):
            kt_ref[block] = kv_ref[block, :, :size].T
        dk_ref[...] = jnp.zeros_like(dk_ref)
        dv_ref[...] = jnp.zeros_like(dv_ref)

    parts = [slice(head * size, (head + 1) * size) for head in range(heads)]
    q = jnp.concatenate([q_ref[:, part] for part in parts], axis=0)
    grad = jnp.concatenate([grad_ref[:, part] for part in parts], axis=0)
    out_t = jnp.concatenate([out_ref[:, part].T for part in parts], axis=1)
    qt, grad_t = q.T, grad.T
    delta = jnp.sum(grad_t.astype(F32) * out_t.astype(F32), axis=0, keepdims=True)
    low, high, lse = low_ref[...], high_ref[...], lse_ref[0]

    def step(block, dq, masked):
        scores = dot(kv_ref[block, :, :size], qt)
        if masked:
            scores = jnp.where(visible(block * keys, keys, low, high), scores, NEGATIVE)
        probs = jnp.exp2(scores - lse)
        probs_grad = dot(kv_ref[block, :, size:], grad_t)
        score_grad = (probs * (probs_grad - delta)).astype(BF16)
        dv_ref[block] += dot(probs.astype(BF16), grad)
        dk_ref[block] += dot(score_grad, q)
        return dq + dot(kt_ref[block], score_grad)

    dq = jnp.zeros((size, heads * rows), F32)
    dq = lax.fori_loop(spans[0], spans[1], functools.partial(step, masked=True), dq)
    dq = lax.fori_loop(spans[2], spans[3], functools.partial(step, masked=False), dq)
    dq = lax.fori_loop(spans[4], spans[5], functools.partial(step, masked=True), dq)
    for head, part in enumerate(parts):
        turned = rotate(dq[:, head * rows : (head + 1) * rows].T, cos_ref[...], -sin_ref[...])
        dq_ref[:, part] = (turned * size ** -0.5).astype(BF16)

    @pl.when(pl.program_id(0) == pl.num_programs(0) - 1)
    def _():
        for block in range(dkv_ref.shape[0]):
            dkv_ref[block, :, :size] = (dk_ref[block] * LN2).astype(BF16)
            dkv_ref[block, :, size:] = dv_ref[block].astype(BF16)


def attention_calls(rows, width, size, count, keys, micro):
    heads = 2 if (width // size) % 2 == 0 else 1
    groups = width // size // heads
    span = heads * size
    head_block = pl.BlockSpec((rows, span), lambda g, s: (0, g))

    def whole(*shape):
        return pl.BlockSpec(shape, lambda g, s: (0,) * len(shape))

    lse_block = pl.BlockSpec((1, 1, heads * rows), lambda g, s: (g, 0, 0))
    shared = [
        head_block,
        pl.BlockSpec((count, keys, 2 * size), lambda g, s: (0, micro, 0)),
        whole(1, heads * rows), whole(1, heads * rows),
        whole(rows, size // 2), whole(rows, size // 2),
    ]
    lse_shape = jax.ShapeDtypeStruct((groups, 1, heads * rows), F32)
    row_shape = jax.ShapeDtypeStruct((rows, width), BF16)
    params = pltpu.CompilerParams(vmem_limit_bytes=48 * 2**20)
    work = rows * width * min(count * keys, WINDOW) * 2
    sizes = dict(heads=heads, size=size, keys=keys)
    forward = pl.pallas_call(
        functools.partial(attend_kernel, **sizes),
        out_shape=(row_shape, row_shape, lse_shape),
        grid_spec=pltpu.PrefetchScalarGridSpec(
            num_scalar_prefetch=1, grid=(groups,), in_specs=shared,
            out_specs=(head_block, head_block, lse_block),
            scratch_shapes=[pltpu.VMEM((count, size, keys), BF16)],
        ),
        compiler_params=params,
        cost_estimate=pl.CostEstimate(
            flops=2 * work, bytes_accessed=rows * width * 8, transcendentals=work // size // 2
        ),
    )
    backward = pl.pallas_call(
        functools.partial(attend_back_kernel, **sizes),
        out_shape=(row_shape, jax.ShapeDtypeStruct((count, keys, 2 * size), BF16)),
        grid_spec=pltpu.PrefetchScalarGridSpec(
            num_scalar_prefetch=1, grid=(groups,),
            in_specs=shared + [head_block, head_block, lse_block],
            out_specs=(head_block, whole(count, keys, 2 * size)),
            scratch_shapes=[
                pltpu.VMEM((count, size, keys), BF16),
                pltpu.VMEM((count, keys, size), F32),
                pltpu.VMEM((count, keys, size), F32),
            ],
        ),
        compiler_params=params,
        cost_estimate=pl.CostEstimate(
            flops=5 * work, bytes_accessed=rows * width * 10, transcendentals=work // size // 2
        ),
    )
    return forward, backward, heads


def pad_rows(array, rows):
    return jnp.pad(array, ((0, rows - array.shape[0]), (0, 0)))


def weight_kernel(a_here, a_there, b_here, b_there, out_ref):
    out_ref[...] = (
        contract_rows(a_here[...], b_here[...]) + contract_rows(a_there[...], b_there[...])
    ).astype(BF16)


def weight_grad(left, right):
    rows, width = left[0].shape
    cols = right[0].shape[1]
    tile = 256 if width % 256 == 0 else 128

    def column(array):
        return pl.BlockSpec((rows, tile), lambda i: (0, i))

    def fixed(array):
        return pl.BlockSpec(array.shape, lambda i: (0, 0), pipeline_mode=pl.Buffered(1))

    return pl.pallas_call(
        weight_kernel,
        out_shape=jax.ShapeDtypeStruct((width, cols), BF16),
        grid=(width // tile,),
        in_specs=[column(a) for a in left] + [fixed(a) for a in right],
        out_specs=pl.BlockSpec((tile, cols), lambda i: (i, 0)),
        compiler_params=pltpu.CompilerParams(vmem_limit_bytes=48 * 2**20),
        cost_estimate=pl.CostEstimate(
            flops=4 * rows * width * cols,
            bytes_accessed=4 * rows * (width + cols) + 2 * width * cols,
            transcendentals=0,
        ),
    )(*left, *right)


def local(
    tokens, segment_ids, cotangent, gain_attn, w_query, w_key, w_value, w_out, gain_mlp,
    w_gate, w_up, w_down,
):
    micros, _, rows, width = tokens.shape
    size = w_key.shape[1]
    query_width = w_query.shape[1]
    hidden_cols = w_gate.shape[1]
    count = lax.axis_size("ctx")
    first = lax.axis_index("ctx") * rows
    padded = -(-rows // 128) * 128
    calls = [
        attention_calls(padded, query_width, size, count, rows, m) for m in range(micros)
    ]
    heads = calls[0][2]
    plan = Plan()

    ids = segment_ids[:, 0]
    slots = w_key.shape[0]
    id_cols = -(-micros * rows // slots)
    id_flat = jnp.pad(ids.reshape(-1), (0, id_cols * slots - micros * rows)).astype(BF16)
    beside = jnp.concatenate(
        [jnp.stack([gain_attn, gain_mlp], axis=1), id_flat.reshape(slots, id_cols)], axis=1
    )
    beside = jnp.pad(beside, ((0, 0), (0, -beside.shape[1] % 128)))
    narrow_in = plan.start(gather_everywhere(jnp.concatenate([w_key, w_value, beside], axis=1)))
    query_in = plan.start(gather_everywhere(w_query))
    gate_in = Whole(plan, ctx_gather, w_gate)
    for _ in range(3):
        plan.step(narrow_in)
    plan.step(query_in)
    plan.step(narrow_in)
    plan.step(narrow_in)
    plan.step(query_in)
    narrow_full, narrow_ring = narrow_in.end()
    w_kv = narrow_full[:, : 2 * size]
    gain_first = narrow_full[:, 2 * size].astype(F32)
    gain_second = narrow_full[:, 2 * size + 1].astype(F32)
    ids_all = narrow_ring[:, :, 2 * size + 2 : 2 * size + 2 + id_cols].reshape(count, -1)
    ids_all = ids_all[:, : micros * rows].reshape(count, micros, rows)
    ids_all = ids_all.transpose(1, 0, 2).reshape(micros, count * rows).astype(jnp.int32)

    index = first + jnp.arange(rows, dtype=jnp.int32)
    half = size // 2

    def tables(index):
        freqs = 10000.0 ** (-jnp.arange(half, dtype=F32) / half)
        angles = index.astype(F32)[:, None] * freqs
        return jnp.cos(angles), jnp.sin(angles)

    cosine, sine = tables(index)
    begins = jnp.sum(
        (ids_all[:, None, :] < ids[:, :, None]).astype(jnp.int32), axis=-1, dtype=jnp.int32
    )
    lowest = jnp.maximum(begins, index[None] - (WINDOW - 1))

    def project_kv(rows_in, gain, weights, cosine, sine):
        normed = rms_scale(rows_in[:, 0].astype(F32), gain).astype(BF16)
        normed = normed.reshape(micros * rows, width)
        both = dot(normed, weights)
        keys = both[:, :size].astype(BF16).astype(F32)
        twice = [jnp.concatenate([t] * micros, axis=0) for t in (cosine, sine)]
        return normed, jnp.concatenate([rotate(keys, *twice), both[:, size:]], axis=1).astype(BF16)

    normed, turned = plan.run(project_kv, tokens, gain_first, w_kv, cosine, sine)
    kv_in = plan.start(ring_gather(turned))
    plan.step(query_in)
    plan.step(kv_in)
    plan.step(query_in)
    out_in = plan.start(gather_everywhere(plan.hold(w_out).T))
    plan.step(kv_in)
    plan.step(query_in)
    cot = plan.hold(cotangent).reshape(micros * rows, width)
    cot_near, cot_far = plan.start(once(core_swap(cot))), plan.start(rows_there(cot))
    plan.step(out_in)
    query_full, _ = query_in.end()
    gate_full = gate_in.end()
    queries = plan.run(lambda a, b: dot(a, b).reshape(micros, rows, -1), normed, query_full)
    plan.step(kv_in)
    plan.step(out_in)

    saved = []
    kv_all = kv_in.end()
    up_in = Whole(plan, ctx_gather, w_up)
    for m in range(micros):
        full_from = (jnp.max(lowest[m]) + rows - 1) // rows
        full_to = (first + 1) // rows
        last = (first + rows - 1) // rows + 1
        spans = jnp.stack([
            jnp.min(lowest[m]) // rows, jnp.minimum(full_from, last),
            full_from, full_to,
            jnp.maximum(full_from, full_to), last,
        ]).astype(jnp.int32)

        def lanes(values):
            return jnp.tile(jnp.pad(values, (0, padded - rows))[None], (1, heads))

        shared = (
            kv_all, lanes(lowest[m]), lanes(index),
            pad_rows(cosine, padded), pad_rows(sine, padded),
        )
        attended, query_rot, lse = plan.run(
            lambda q, s, *rest: calls[m][0](s, q, *rest),
            pad_rows(queries[m], padded), spans, *shared,
        )
        saved.append((spans, query_rot, shared, attended, lse))
        plan.step(out_in)

    attended = jnp.concatenate([entry[3][:rows] for entry in saved], axis=0)
    out_full, _ = out_in.end()

    def join(attended, tokens, weights, gain):
        middle = tokens.reshape(micros * rows, width).astype(F32) + contract_last(attended, weights)
        return middle, rms_scale(middle, gain).astype(BF16)

    middle, low = plan.run(join, attended, tokens, out_full, gain_second)
    near_in, far_in = plan.start(once(core_swap(low))), plan.start(rows_there(low))

    plan.step(cot_near)
    normed_rows = [jnp.concatenate([low, near_in.end()], axis=0)]
    gate_rows = [plan.run(dot, normed_rows[0], gate_full)]
    cot_rows = [jnp.concatenate([cot, cot_near.end()], axis=0)]
    up_full = up_in.end()
    down_in = Whole(plan, ctx_gather, w_down.T)

    def make_hidden(rows_in, weights, gate):
        up = dot(rows_in, weights)
        return up, (jax.nn.gelu(gate) * up).astype(BF16)

    up_rows, hidden = [], []

    def hidden_half(side):
        up, both = plan.run(make_hidden, normed_rows[side], up_full, gate_rows[side])
        up_rows.append(up)
        hidden.append(both)

    hidden_half(0)
    plan.step(far_in)
    normed_rows.append(jnp.concatenate(far_in.end(), axis=0))
    gate_rows.append(plan.run(dot, normed_rows[1], gate_full))
    hidden_half(1)
    plan.step(cot_far)
    cot_rows.append(jnp.concatenate(cot_far.end(), axis=0))

    def weight_sum(left, right):
        terms = plan.run(lambda a, *rest: weight_grad((a, left[1]), right), left[0])
        return Whole(plan, ctx_scatter, terms)

    down_out = weight_sum(cot_rows, hidden)
    down_full = down_in.end()

    def both_halves(function, parts, between=None):
        there = plan.start(scatter_there(function(1), parts))
        if between is not None:
            between()
        here = plan.start(scatter_here(function(0)))
        plan.step(there)
        return here, there

    mlp_here, mlp_there = both_halves(
        lambda side: plan.run(lambda a, b: contract_last(a, b, BF16), hidden[side], down_full), 1
    )

    def hidden_back(cot, weights, gate, up):
        hidden_grad = dot(cot, weights)
        gelu_gate, gelu_back = jax.vjp(jax.nn.gelu, gate)
        gate_grad = gelu_back(hidden_grad * up)[0].astype(BF16)
        return gate_grad, (hidden_grad * gelu_gate).astype(BF16)

    gate_grad, up_grad = [None, None], [None, None]
    for side in range(2):
        gate_grad[side], up_grad[side] = plan.run(
            hidden_back, cot_rows[side], down_full, gate_rows[side], up_rows[side]
        )
    mlp_own = mlp_here.end()
    gate_out = weight_sum(normed_rows, gate_grad)
    mlp_came = mlp_there.end()

    def rows_back(side):
        part = plan.run(contract_last, gate_grad[side], gate_full)
        return plan.run(
            lambda a, b, c: (contract_last(a, b) + c).astype(BF16), up_grad[side], up_full, part
        )

    back_here, back_there = both_halves(rows_back, micros, down_out.end)
    up_out = weight_sum(normed_rows, up_grad)

    middle_grads, branch_grads, attended_grads, gain_two = [], [], [], []
    query_grads, kv_out = [], []
    back_own = back_here.end()

    def join_back(came, own, middle, gain, cot):
        incoming = own + came.astype(F32)
        middle_part, gain_part = jax.vjp(rms_scale, middle, gain)[1](incoming)
        middle_grad = middle_part + cot.astype(F32)
        return middle_grad, middle_grad.astype(BF16), gain_part

    def before_attention(m):
        here = slice(m * rows, (m + 1) * rows)
        middle_grad, branch_grad, gain_part = plan.run(
            join_back, back_there.passed[m], back_own[here], middle[here], gain_second, cot[here]
        )
        middle_grads.append(middle_grad)
        branch_grads.append(branch_grad)
        gain_two.append(gain_part)
        attended_grads.append(plan.run(lambda a, b: dot(a, b, BF16), branch_grad, out_full))

    def through_attention(m):
        spans, query_rot, shared, attended, lse = saved[m]
        query_grad, kv_term = plan.run(
            lambda g, s, q, shared, out, lse: calls[m][1](s, q, *shared, out, g, lse),
            pad_rows(attended_grads[m], padded), spans, query_rot, shared, attended, lse,
        )
        query_grads.append(query_grad[:rows])
        kv_out.append(plan.start(ring_scatter(kv_term)))

    plan.step(back_there)
    before_attention(0)
    through_attention(0)
    gate_out.end()
    plan.step(back_there)
    before_attention(1)
    plan.step(kv_out[0])
    out_out = plan.start(scatter_everywhere(
        plan.run(
            lambda a, b: contract_rows(a, b, BF16), jnp.concatenate(branch_grads, axis=0), attended
        )
    ))
    plan.step(kv_out[0])
    through_attention(1)
    plan.step(out_out)
    plan.step(kv_out[0])
    query_grad = jnp.concatenate(query_grads, axis=0)
    query_out = plan.start(scatter_everywhere(
        plan.run(lambda a, b: contract_rows(a, b, BF16), normed, query_grad)
    ))
    plan.step(kv_out[0])
    plan.step(kv_out[1])
    part = plan.run(contract_last, query_grad, query_full)
    plan.step(query_out)
    plan.step(kv_out[1])

    def finish_output(came, own, middle):
        return (middle + own + came.astype(F32)).reshape(micros, rows, width)

    output = plan.run(finish_output, mlp_came, mlp_own, middle)
    plan.step(kv_out[1])
    plan.step(out_out)
    kv_own = jnp.concatenate([t.end() for t in kv_out], axis=0)
    twice = [jnp.concatenate([t] * micros, axis=0) for t in (cosine, sine)]
    key_own = rotate(kv_own[:, :size], twice[0], -twice[1])
    kv_grad = jnp.concatenate([key_own, kv_own[:, size:]], axis=1).astype(BF16)

    def narrow_back(kv_grad, normed):
        return contract_rows(normed, kv_grad, BF16)

    def inputs_back(kv_grad, part, weights, tokens, gain, middle_grads):
        attn_in_grad = part + contract_last(kv_grad, weights)
        norm_back = jax.vjp(rms_scale, tokens[:, 0].astype(F32), gain)[1]
        input_part, gain_one = norm_back(attn_in_grad.reshape(micros, rows, width))
        return jnp.stack(middle_grads) + input_part, gain_one

    kv_terms = plan.run(narrow_back, kv_grad, normed)
    grad_tokens, gain_one = plan.run(
        inputs_back, kv_grad, part, w_kv, tokens, gain_first, middle_grads
    )
    gain_cols = jnp.stack([gain_one, sum(gain_two)], axis=1).astype(BF16)
    narrow_out = plan.start(scatter_everywhere(
        jnp.concatenate([kv_terms, jnp.pad(gain_cols, ((0, 0), (0, 126)))], axis=1)
    ))
    for _ in range(count):
        plan.step(narrow_out, out_out, query_out)
    narrow_grad = narrow_out.end()
    return (
        output[:, None],
        grad_tokens[:, None],
        narrow_grad[:, 2 * size],
        query_out.end(),
        narrow_grad[:, :size],
        narrow_grad[:, size : 2 * size],
        out_out.end().T,
        narrow_grad[:, 2 * size + 1],
        gate_out.value.astype(F32),
        up_out.end().astype(F32),
        down_out.value.T.astype(F32),
    )


def solution(mesh):
    rows = P(None, "wt", "ctx", None)
    everywhere = P(("ctx", "wt"))
    tall = P(("ctx", "wt"), None)
    wide = P(None, ("ctx", "wt"))
    square = P("ctx", "wt")
    return jax.shard_map(
        local,
        mesh=mesh,
        in_specs=(
            rows, P(None, "wt", "ctx"), rows, everywhere, tall, tall, tall, wide, everywhere,
            square, square, P("wt", "ctx"),
        ),
        out_specs=(
            rows, rows, everywhere, tall, tall, tall, wide, everywhere, square, square,
            P("wt", "ctx"),
        ),
        check_vma=False,
    )
```

```python
import functools
import math

import jax
import jax.numpy as jnp
from jax import lax
from jax.experimental import pallas as pl
from jax.experimental.pallas import tpu as pltpu
from jax.sharding import PartitionSpec as P

WINDOW = 2048
EPSILON = 1e-06
NEGATIVE = -1e30
LOG2E = math.log2(math.e)
LN2 = math.log(2.0)
F32 = jnp.float32
BF16 = jnp.bfloat16


def rms_scale(values, gain):
    return values * lax.rsqrt(jnp.mean(values * values, axis=-1, keepdims=True) + EPSILON) * gain


def dot(left, right, out=F32):
    return jnp.dot(left, right, preferred_element_type=out)


def contract_rows(left, right, out=F32):
    return lax.dot_general(left, right, (((0,), (0,)), ((), ())), preferred_element_type=out)


def contract_last(left, right, out=F32):
    return lax.dot_general(left, right, (((1,), (1,)), ((), ())), preferred_element_type=out)


class Plan:
    def __init__(self):
        self.now = ()

    def hold(self, value):
        if not self.now:
            return value
        return lax.optimization_barrier((value,) + self.now)[0]

    def run(self, function, first, *rest):
        out = function(self.hold(first), *rest)
        self.now = tuple(jax.tree.leaves(out))
        return out

    def start(self, generator):
        return Transfer(self, generator)

    def step(self, *transfers):
        for transfer in transfers:
            transfer.step()


class Transfer:
    def __init__(self, plan, generator):
        self.plan, self.generator = plan, generator
        self.ended, self.value, self.passed = False, None, []
        self.launch(None)

    def launch(self, arrived):
        try:
            wanted = self.generator.send(arrived)
            while not isinstance(wanted, list):
                self.passed.append(wanted)
                wanted = next(self.generator)
        except StopIteration as stop:
            self.ended, self.value = True, stop.value
            return
        held = [self.plan.hold(operand) for operand, _, _ in wanted]
        self.flying = [
            lax.ppermute(operand, axis, pairs) for operand, (_, axis, pairs) in zip(held, wanted)
        ]
        self.plan.now = self.plan.now + tuple(operand for operand, _, _ in wanted)

    def step(self):
        if not self.ended:
            arrived = self.flying
            self.plan.now = self.plan.now + tuple(arrived)
            self.launch(arrived)

    def end(self):
        while not self.ended:
            self.step()
        return self.value


class Whole:
    def __init__(self, plan, function, operand):
        self.plan, self.value = plan, function(plan.hold(operand))

    def end(self):
        self.plan.now = self.plan.now + (self.value,)
        return self.value


def ctx_gather(block):
    return lax.all_gather(block, "ctx", axis=0, tiled=True)


def ctx_scatter(terms):
    return lax.psum_scatter(terms, "ctx", scatter_dimension=0, tiled=True)


def ring_order(count):
    return list(range(0, count, 2)) + [i for i in range(count - 1, 0, -1) if i % 2]


def ring(block, shift):
    count = lax.axis_size("ctx")
    order = ring_order(count)
    return block, "ctx", [(order[i], order[(i + shift) % count]) for i in range(count)]


def wt_swap(block, bit):
    return block, "wt", [(i, i ^ bit) for i in range(lax.axis_size("wt"))]


def core_swap(block):
    return wt_swap(block, 1)


def x_swap(block):
    return wt_swap(block, 2)


def ring_index(offset):
    count = lax.axis_size("ctx")
    here = lax.axis_index("ctx")
    place = jnp.where(here % 2 == 0, here // 2, count - 1 - here // 2)
    place = (place + offset + count) % count
    return jnp.where(place < count // 2, 2 * place, 2 * (count - 1 - place) + 1)


def half_rows(rows):
    return rows // 2 // 16 * 16 if rows >= 32 else rows // 2


def ring_blocks(block):
    half = lax.axis_size("ctx") // 2
    cut = half_rows(block.shape[0])
    ahead = behind = block
    for step in range(1, half):
        ahead, behind = yield [ring(ahead, 1), ring(behind, -1)], None
        yield None, [(-step, 0, ahead), (step, 0, behind)]
    low, high = yield [ring(ahead[:cut], 1), ring(behind[cut:], -1)], None
    yield None, [(half, 0, low), (half, cut, high)]


def put(found, piece, offset, row):
    start = (ring_index(offset), row) + (0,) * (piece.ndim - 1)
    return lax.dynamic_update_slice(found, piece[None], start)


def begin_kernel(place, block_ref, out_ref):
    del place
    out_ref[0] = block_ref[...]


def begin(block, count):
    shape = block.shape
    return pl.pallas_call(
        begin_kernel,
        out_shape=jax.ShapeDtypeStruct((count,) + shape, block.dtype),
        grid_spec=pltpu.PrefetchScalarGridSpec(
            num_scalar_prefetch=1,
            grid=(1,),
            in_specs=[pl.BlockSpec(shape, lambda i, place: (0, 0))],
            out_specs=pl.BlockSpec((1,) + shape, lambda i, place: (place[0], 0, 0)),
        ),
        cost_estimate=pl.CostEstimate(
            flops=0, bytes_accessed=4 * math.prod(shape), transcendentals=0
        ),
    )(lax.axis_index("ctx").reshape(1), block)


def ring_gather(block):
    found = begin(block, lax.axis_size("ctx"))
    blocks = ring_blocks(block)
    wanted, _ = next(blocks)
    while wanted is not None:
        arrived = yield wanted
        _, pieces = blocks.send(arrived)
        for offset, row, piece in pieces:
            found = put(found, piece, offset, row)
        wanted, _ = next(blocks, (None, None))
    return found


def ring_scatter(terms):
    half = terms.shape[0] // 2
    cut = half_rows(terms.shape[1])

    def own(offset):
        return lax.dynamic_index_in_dim(terms, ring_index(offset), 0, keepdims=False)

    far = own(half)
    ahead, behind = yield [ring(far[:cut], 1), ring(far[cut:], -1)]
    if half == 1:
        return own(0).astype(F32) + jnp.concatenate([ahead, behind], axis=0).astype(F32)
    for step in range(half - 1, 0, -1):
        up, down = own(step), own(-step)
        if step == half - 1:
            up = jnp.concatenate([add(up[:cut], ahead), up[cut:]], axis=0)
            down = jnp.concatenate([down[:cut], add(down[cut:], behind)], axis=0)
        else:
            up, down = add(up, ahead), add(down, behind)
        ahead, behind = yield [ring(up, 1), ring(down, -1)]
    return own(0).astype(F32) + ahead.astype(F32) + behind.astype(F32)


def add(first, second):
    return (first.astype(F32) + second.astype(F32)).astype(BF16)


def gather_everywhere(block):
    here = lax.axis_index("wt")
    width = block.shape[1]
    mine = begin(block, lax.axis_size("ctx"))
    far = None
    blocks = ring_blocks(block)
    crossing = [(0, 0, block)]
    wanted, _ = next(blocks)
    while wanted is not None or crossing:
        turns = wanted or []
        arrived = yield turns + [x_swap(piece) for _, _, piece in crossing]
        for (offset, row, _), piece in zip(crossing, arrived[len(turns) :]):
            far = begin(piece, mine.shape[0]) if far is None else put(far, piece, offset, row)
        crossing = []
        if wanted is not None:
            _, crossing = blocks.send(arrived[: len(turns)])
            for offset, row, piece in crossing:
                mine = put(mine, piece, offset, row)
            wanted, _ = next(blocks, (None, None))
    near, last = yield [core_swap(mine), core_swap(far)]
    return interleave(here, mine, near, far, last).reshape(-1, width), mine


def interleave_kernel(here, *refs):
    *pieces, out_ref = refs
    for bit, piece in enumerate(pieces):
        out_ref[0, here[0] ^ bit] = piece[0]


def interleave(here, *pieces):
    count, rows, width = pieces[0].shape
    return pl.pallas_call(
        interleave_kernel,
        out_shape=jax.ShapeDtypeStruct((count, 4, rows, width), pieces[0].dtype),
        grid_spec=pltpu.PrefetchScalarGridSpec(
            num_scalar_prefetch=1,
            grid=(count,),
            in_specs=[pl.BlockSpec((1, rows, width), lambda i, here: (i, 0, 0))] * 4,
            out_specs=pl.BlockSpec((1, 4, rows, width), lambda i, here: (i, 0, 0, 0)),
        ),
        cost_estimate=pl.CostEstimate(
            flops=0, bytes_accessed=16 * count * rows * width, transcendentals=0
        ),
    )(here.reshape(1), *pieces)


def scatter_everywhere(terms):
    here = lax.axis_index("wt")
    count = lax.axis_size("ctx")
    rows = terms.shape[0] // (4 * count)
    split = terms.reshape(count, 2, 2, rows, terms.shape[1])
    x_here, core_here = here // 2, here % 2
    sent = lax.dynamic_index_in_dim(split, 1 - core_here, 2, keepdims=False)
    (came,) = yield [core_swap(sent)]
    both = add(lax.dynamic_index_in_dim(split, core_here, 2, keepdims=False), came)
    sent = lax.dynamic_index_in_dim(both, 1 - x_here, 1, keepdims=False)
    (came,) = yield [x_swap(sent)]
    kept = add(lax.dynamic_index_in_dim(both, x_here, 1, keepdims=False), came)
    return (yield from ring_scatter(kept))


def once(permute):
    (came,) = yield [permute]
    return came


def rows_there(block):
    (far,) = yield [x_swap(block)]
    (last,) = yield [core_swap(far)]
    return [far, last]


def scatter_here(terms):
    rows = terms.shape[0] // 2
    (near,) = yield [core_swap(terms[rows:])]
    return terms[:rows].astype(F32) + near.astype(F32)


def scatter_there(terms, parts):
    rows = terms.shape[0] // 2
    (last,) = yield [core_swap(terms[rows:])]
    far = add(terms[:rows], last)
    came = []
    for part in jnp.split(far, parts):
        came += yield [x_swap(part)]
        yield came[-1]
    return jnp.concatenate(came, axis=0)


def rotate(values, cosine, sine):
    half = values.shape[-1] // 2
    first, second = values[:, :half], values[:, half:]
    return jnp.concatenate(
        [first * cosine - second * sine, second * cosine + first * sine], axis=-1
    )


def visible(start, keys, low, high):
    index = start + lax.broadcasted_iota(jnp.int32, (keys, low.shape[1]), 0)
    return (index >= low) & (index <= high)


def attend_kernel(
    spans, q_ref, kv_ref, low_ref, high_ref, cos_ref, sin_ref,
    out_ref, qrot_ref, lse_ref, vt_ref, *, heads, size, keys,
):
    rows = q_ref.shape[0]
    scale = size ** -0.5 * LOG2E

    @pl.when(pl.program_id(0) == 0)
    def _():
        for block in range(kv_ref.shape[0]):
            vt_ref[block] = kv_ref[block, :, size:].T

    turned = []
    for head in range(heads):
        part = rotate(q_ref[:, head * size : (head + 1) * size], cos_ref[...], sin_ref[...])
        part = (part * scale).astype(BF16)
        qrot_ref[:, head * size : (head + 1) * size] = part
        turned.append(part.T)
    qt = jnp.concatenate(turned, axis=1)
    low, high = low_ref[...], high_ref[...]

    def step(block, carry, masked):
        top, total, acc = carry
        scores = dot(kv_ref[block, :, :size], qt)
        if masked:
            scores = jnp.where(visible(block * keys, keys, low, high), scores, NEGATIVE)
        new_top = jnp.maximum(top, jnp.max(scores, axis=0, keepdims=True))
        probs = jnp.exp2(scores - new_top)
        fade = jnp.exp2(top - new_top)
        total = total * fade + jnp.sum(probs, axis=0, keepdims=True)
        acc = acc * fade + dot(vt_ref[block], probs.astype(BF16))
        return new_top, total, acc

    carry = (
        jnp.full((1, heads * rows), NEGATIVE, F32),
        jnp.zeros((1, heads * rows), F32),
        jnp.zeros((size, heads * rows), F32),
    )
    carry = lax.fori_loop(spans[0], spans[1], functools.partial(step, masked=True), carry)
    carry = lax.fori_loop(spans[2], spans[3], functools.partial(step, masked=False), carry)
    carry = lax.fori_loop(spans[4], spans[5], functools.partial(step, masked=True), carry)
    top, total, acc = carry
    acc = acc * (1.0 / total)
    lse_ref[0] = top + jnp.log2(total)
    for head in range(heads):
        out_ref[:, head * size : (head + 1) * size] = (
            acc[:, head * rows : (head + 1) * rows].astype(BF16).T
        )


def attend_back_kernel(
    spans, q_ref, kv_ref, low_ref, high_ref, cos_ref, sin_ref, out_ref, grad_ref, lse_ref,
    dq_ref, dkv_ref, kt_ref, dk_ref, dv_ref, *, heads, size, keys,
):
    rows = q_ref.shape[0]

    @pl.when(pl.program_id(0) == 0)
    def _():
        for block in range(kv_ref.shape[0]):
            kt_ref[block] = kv_ref[block, :, :size].T
        dk_ref[...] = jnp.zeros_like(dk_ref)
        dv_ref[...] = jnp.zeros_like(dv_ref)

    parts = [slice(head * size, (head + 1) * size) for head in range(heads)]
    q = jnp.concatenate([q_ref[:, part] for part in parts], axis=0)
    grad = jnp.concatenate([grad_ref[:, part] for part in parts], axis=0)
    out_t = jnp.concatenate([out_ref[:, part].T for part in parts], axis=1)
    qt, grad_t = q.T, grad.T
    delta = jnp.sum(grad_t.astype(F32) * out_t.astype(F32), axis=0, keepdims=True)
    low, high, lse = low_ref[...], high_ref[...], lse_ref[0]

    def step(block, dq, masked):
        scores = dot(kv_ref[block, :, :size], qt)
        if masked:
            scores = jnp.where(visible(block * keys, keys, low, high), scores, NEGATIVE)
        probs = jnp.exp2(scores - lse)
        probs_grad = dot(kv_ref[block, :, size:], grad_t)
        score_grad = (probs * (probs_grad - delta)).astype(BF16)
        dv_ref[block] += dot(probs.astype(BF16), grad)
        dk_ref[block] += dot(score_grad, q)
        return dq + dot(kt_ref[block], score_grad)

    dq = jnp.zeros((size, heads * rows), F32)
    dq = lax.fori_loop(spans[0], spans[1], functools.partial(step, masked=True), dq)
    dq = lax.fori_loop(spans[2], spans[3], functools.partial(step, masked=False), dq)
    dq = lax.fori_loop(spans[4], spans[5], functools.partial(step, masked=True), dq)
    for head, part in enumerate(parts):
        turned = rotate(dq[:, head * rows : (head + 1) * rows].T, cos_ref[...], -sin_ref[...])
        dq_ref[:, part] = (turned * size ** -0.5).astype(BF16)

    @pl.when(pl.program_id(0) == pl.num_programs(0) - 1)
    def _():
        for block in range(dkv_ref.shape[0]):
            dkv_ref[block, :, :size] = (dk_ref[block] * LN2).astype(BF16)
            dkv_ref[block, :, size:] = dv_ref[block].astype(BF16)


def attention_calls(rows, width, size, count, keys, micro):
    heads = 2 if (width // size) % 2 == 0 else 1
    groups = width // size // heads
    span = heads * size
    head_block = pl.BlockSpec((rows, span), lambda g, s: (0, g))

    def whole(*shape):
        return pl.BlockSpec(shape, lambda g, s: (0,) * len(shape))

    lse_block = pl.BlockSpec((1, 1, heads * rows), lambda g, s: (g, 0, 0))
    shared = [
        head_block,
        pl.BlockSpec((count, keys, 2 * size), lambda g, s: (0, micro, 0)),
        whole(1, heads * rows), whole(1, heads * rows),
        whole(rows, size // 2), whole(rows, size // 2),
    ]
    lse_shape = jax.ShapeDtypeStruct((groups, 1, heads * rows), F32)
    row_shape = jax.ShapeDtypeStruct((rows, width), BF16)
    params = pltpu.CompilerParams(vmem_limit_bytes=48 * 2**20)
    work = rows * width * min(count * keys, WINDOW) * 2
    sizes = dict(heads=heads, size=size, keys=keys)
    forward = pl.pallas_call(
        functools.partial(attend_kernel, **sizes),
        out_shape=(row_shape, row_shape, lse_shape),
        grid_spec=pltpu.PrefetchScalarGridSpec(
            num_scalar_prefetch=1, grid=(groups,), in_specs=shared,
            out_specs=(head_block, head_block, lse_block),
            scratch_shapes=[pltpu.VMEM((count, size, keys), BF16)],
        ),
        compiler_params=params,
        cost_estimate=pl.CostEstimate(
            flops=2 * work, bytes_accessed=rows * width * 8, transcendentals=work // size // 2
        ),
    )
    backward = pl.pallas_call(
        functools.partial(attend_back_kernel, **sizes),
        out_shape=(row_shape, jax.ShapeDtypeStruct((count, keys, 2 * size), BF16)),
        grid_spec=pltpu.PrefetchScalarGridSpec(
            num_scalar_prefetch=1, grid=(groups,),
            in_specs=shared + [head_block, head_block, lse_block],
            out_specs=(head_block, whole(count, keys, 2 * size)),
            scratch_shapes=[
                pltpu.VMEM((count, size, keys), BF16),
                pltpu.VMEM((count, keys, size), F32),
                pltpu.VMEM((count, keys, size), F32),
            ],
        ),
        compiler_params=params,
        cost_estimate=pl.CostEstimate(
            flops=5 * work, bytes_accessed=rows * width * 10, transcendentals=work // size // 2
        ),
    )
    return forward, backward, heads


def pad_rows(array, rows):
    return jnp.pad(array, ((0, rows - array.shape[0]), (0, 0)))


def weight_kernel(a_here, a_there, b_here, b_there, out_ref):
    out_ref[...] = (
        contract_rows(a_here[...], b_here[...]) + contract_rows(a_there[...], b_there[...])
    ).astype(BF16)


def weight_grad(left, right):
    rows, width = left[0].shape
    cols = right[0].shape[1]
    tile = 256 if width % 256 == 0 else 128

    def column(array):
        return pl.BlockSpec((rows, tile), lambda i: (0, i))

    def fixed(array):
        return pl.BlockSpec(array.shape, lambda i: (0, 0), pipeline_mode=pl.Buffered(1))

    return pl.pallas_call(
        weight_kernel,
        out_shape=jax.ShapeDtypeStruct((width, cols), BF16),
        grid=(width // tile,),
        in_specs=[column(a) for a in left] + [fixed(a) for a in right],
        out_specs=pl.BlockSpec((tile, cols), lambda i: (i, 0)),
        compiler_params=pltpu.CompilerParams(vmem_limit_bytes=48 * 2**20),
        cost_estimate=pl.CostEstimate(
            flops=4 * rows * width * cols,
            bytes_accessed=4 * rows * (width + cols) + 2 * width * cols,
            transcendentals=0,
        ),
    )(*left, *right)


def local(
    tokens, segment_ids, cotangent, gain_attn, w_query, w_key, w_value, w_out, gain_mlp,
    w_gate, w_up, w_down,
):
    micros, _, rows, width = tokens.shape
    size = w_key.shape[1]
    query_width = w_query.shape[1]
    hidden_cols = w_gate.shape[1]
    count = lax.axis_size("ctx")
    first = lax.axis_index("ctx") * rows
    padded = -(-rows // 128) * 128
    calls = [
        attention_calls(padded, query_width, size, count, rows, m) for m in range(micros)
    ]
    heads = calls[0][2]
    plan = Plan()

    ids = segment_ids[:, 0]
    slots = w_key.shape[0]
    id_cols = -(-micros * rows // slots)
    id_flat = jnp.pad(ids.reshape(-1), (0, id_cols * slots - micros * rows)).astype(BF16)
    beside = jnp.concatenate(
        [jnp.stack([gain_attn, gain_mlp], axis=1), id_flat.reshape(slots, id_cols)], axis=1
    )
    beside = jnp.pad(beside, ((0, 0), (0, -beside.shape[1] % 128)))
    narrow_in = plan.start(gather_everywhere(jnp.concatenate([w_key, w_value, beside], axis=1)))
    query_in = plan.start(gather_everywhere(w_query))
    gate_in = Whole(plan, ctx_gather, w_gate)
    for _ in range(3):
        plan.step(narrow_in)
    plan.step(query_in)
    plan.step(narrow_in)
    plan.step(narrow_in)
    plan.step(query_in)
    narrow_full, narrow_ring = narrow_in.end()
    w_kv = narrow_full[:, : 2 * size]
    gain_first = narrow_full[:, 2 * size].astype(F32)
    gain_second = narrow_full[:, 2 * size + 1].astype(F32)
    ids_all = narrow_ring[:, :, 2 * size + 2 : 2 * size + 2 + id_cols].reshape(count, -1)
    ids_all = ids_all[:, : micros * rows].reshape(count, micros, rows)
    ids_all = ids_all.transpose(1, 0, 2).reshape(micros, count * rows).astype(jnp.int32)

    index = first + jnp.arange(rows, dtype=jnp.int32)
    half = size // 2

    def tables(index):
        freqs = 10000.0 ** (-jnp.arange(half, dtype=F32) / half)
        angles = index.astype(F32)[:, None] * freqs
        return jnp.cos(angles), jnp.sin(angles)

    cosine, sine = tables(index)
    begins = jnp.sum(
        (ids_all[:, None, :] < ids[:, :, None]).astype(jnp.int32), axis=-1, dtype=jnp.int32
    )
    lowest = jnp.maximum(begins, index[None] - (WINDOW - 1))

    def project_kv(rows_in, gain, weights, cosine, sine):
        normed = rms_scale(rows_in[:, 0].astype(F32), gain).astype(BF16)
        normed = normed.reshape(micros * rows, width)
        both = dot(normed, weights)
        keys = both[:, :size].astype(BF16).astype(F32)
        twice = [jnp.concatenate([t] * micros, axis=0) for t in (cosine, sine)]
        return normed, jnp.concatenate([rotate(keys, *twice), both[:, size:]], axis=1).astype(BF16)

    normed, turned = plan.run(project_kv, tokens, gain_first, w_kv, cosine, sine)
    kv_in = plan.start(ring_gather(turned))
    plan.step(query_in)
    plan.step(kv_in)
    plan.step(query_in)
    out_in = plan.start(gather_everywhere(plan.hold(w_out).T))
    plan.step(kv_in)
    plan.step(query_in)
    cot = plan.hold(cotangent).reshape(micros * rows, width)
    cot_near, cot_far = plan.start(once(core_swap(cot))), plan.start(rows_there(cot))
    plan.step(out_in)
    query_full, _ = query_in.end()
    gate_full = gate_in.end()
    queries = plan.run(lambda a, b: dot(a, b).reshape(micros, rows, -1), normed, query_full)
    plan.step(kv_in)
    plan.step(out_in)

    saved = []
    kv_all = kv_in.end()
    up_in = Whole(plan, ctx_gather, w_up)
    for m in range(micros):
        full_from = (jnp.max(lowest[m]) + rows - 1) // rows
        full_to = (first + 1) // rows
        last = (first + rows - 1) // rows + 1
        spans = jnp.stack([
            jnp.min(lowest[m]) // rows, jnp.minimum(full_from, last),
            full_from, full_to,
            jnp.maximum(full_from, full_to), last,
        ]).astype(jnp.int32)

        def lanes(values):
            return jnp.tile(jnp.pad(values, (0, padded - rows))[None], (1, heads))

        shared = (
            kv_all, lanes(lowest[m]), lanes(index),
            pad_rows(cosine, padded), pad_rows(sine, padded),
        )
        attended, query_rot, lse = plan.run(
            lambda q, s, *rest: calls[m][0](s, q, *rest),
            pad_rows(queries[m], padded), spans, *shared,
        )
        saved.append((spans, query_rot, shared, attended, lse))
        plan.step(out_in)

    attended = jnp.concatenate([entry[3][:rows] for entry in saved], axis=0)
    out_full, _ = out_in.end()

    def join(attended, tokens, weights, gain):
        middle = tokens.reshape(micros * rows, width).astype(F32) + contract_last(attended, weights)
        return middle, rms_scale(middle, gain).astype(BF16)

    middle, low = plan.run(join, attended, tokens, out_full, gain_second)
    near_in, far_in = plan.start(once(core_swap(low))), plan.start(rows_there(low))

    plan.step(cot_near)
    normed_rows = [jnp.concatenate([low, near_in.end()], axis=0)]
    gate_rows = [plan.run(dot, normed_rows[0], gate_full)]
    cot_rows = [jnp.concatenate([cot, cot_near.end()], axis=0)]
    up_full = up_in.end()
    down_in = Whole(plan, ctx_gather, w_down.T)

    def make_hidden(rows_in, weights, gate):
        up = dot(rows_in, weights)
        return up, (jax.nn.gelu(gate) * up).astype(BF16)

    up_rows, hidden = [], []

    def hidden_half(side):
        up, both = plan.run(make_hidden, normed_rows[side], up_full, gate_rows[side])
        up_rows.append(up)
        hidden.append(both)

    hidden_half(0)
    plan.step(far_in)
    normed_rows.append(jnp.concatenate(far_in.end(), axis=0))
    gate_rows.append(plan.run(dot, normed_rows[1], gate_full))
    hidden_half(1)
    plan.step(cot_far)
    cot_rows.append(jnp.concatenate(cot_far.end(), axis=0))

    def weight_sum(left, right):
        terms = plan.run(lambda a, *rest: weight_grad((a, left[1]), right), left[0])
        return Whole(plan, ctx_scatter, terms)

    down_out = weight_sum(cot_rows, hidden)
    down_full = down_in.end()

    def both_halves(function, parts, between=None):
        there = plan.start(scatter_there(function(1), parts))
        if between is not None:
            between()
        here = plan.start(scatter_here(function(0)))
        plan.step(there)
        return here, there

    mlp_here, mlp_there = both_halves(
        lambda side: plan.run(lambda a, b: contract_last(a, b, BF16), hidden[side], down_full), 1
    )

    def hidden_back(cot, weights, gate, up):
        hidden_grad = dot(cot, weights)
        gelu_gate, gelu_back = jax.vjp(jax.nn.gelu, gate)
        gate_grad = gelu_back(hidden_grad * up)[0].astype(BF16)
        return gate_grad, (hidden_grad * gelu_gate).astype(BF16)

    gate_grad, up_grad = [None, None], [None, None]
    for side in range(2):
        gate_grad[side], up_grad[side] = plan.run(
            hidden_back, cot_rows[side], down_full, gate_rows[side], up_rows[side]
        )
    mlp_own = mlp_here.end()
    gate_out = weight_sum(normed_rows, gate_grad)
    mlp_came = mlp_there.end()

    def rows_back(side):
        part = plan.run(contract_last, gate_grad[side], gate_full)
        return plan.run(
            lambda a, b, c: (contract_last(a, b) + c).astype(BF16), up_grad[side], up_full, part
        )

    back_here, back_there = both_halves(rows_back, micros, down_out.end)
    up_out = weight_sum(normed_rows, up_grad)

    middle_grads, branch_grads, attended_grads, gain_two = [], [], [], []
    query_grads, kv_out = [], []
    back_own = back_here.end()

    def join_back(came, own, middle, gain, cot):
        incoming = own + came.astype(F32)
        middle_part, gain_part = jax.vjp(rms_scale, middle, gain)[1](incoming)
        middle_grad = middle_part + cot.astype(F32)
        return middle_grad, middle_grad.astype(BF16), gain_part

    def before_attention(m):
        here = slice(m * rows, (m + 1) * rows)
        middle_grad, branch_grad, gain_part = plan.run(
            join_back, back_there.passed[m], back_own[here], middle[here], gain_second, cot[here]
        )
        middle_grads.append(middle_grad)
        branch_grads.append(branch_grad)
        gain_two.append(gain_part)
        attended_grads.append(plan.run(lambda a, b: dot(a, b, BF16), branch_grad, out_full))

    def through_attention(m):
        spans, query_rot, shared, attended, lse = saved[m]
        query_grad, kv_term = plan.run(
            lambda g, s, q, shared, out, lse: calls[m][1](s, q, *shared, out, g, lse),
            pad_rows(attended_grads[m], padded), spans, query_rot, shared, attended, lse,
        )
        query_grads.append(query_grad[:rows])
        kv_out.append(plan.start(ring_scatter(kv_term)))

    plan.step(back_there)
    gate_out.end()
    before_attention(0)
    through_attention(0)
    plan.step(back_there)
    before_attention(1)
    plan.step(kv_out[0])
    out_out = plan.start(scatter_everywhere(
        plan.run(
            lambda a, b: contract_rows(a, b, BF16), jnp.concatenate(branch_grads, axis=0), attended
        )
    ))
    plan.step(kv_out[0])
    through_attention(1)
    up_out.end()
    plan.step(out_out)
    plan.step(kv_out[0])
    query_grad = jnp.concatenate(query_grads, axis=0)
    query_out = plan.start(scatter_everywhere(
        plan.run(lambda a, b: contract_rows(a, b, BF16), normed, query_grad)
    ))
    plan.step(kv_out[0])
    plan.step(kv_out[1])
    part = plan.run(contract_last, query_grad, query_full)
    plan.step(query_out)
    plan.step(kv_out[1])

    def finish_output(came, own, middle):
        return (middle + own + came.astype(F32)).reshape(micros, rows, width)

    output = plan.run(finish_output, mlp_came, mlp_own, middle)
    plan.step(kv_out[1])
    plan.step(out_out)
    kv_own = jnp.concatenate([t.end() for t in kv_out], axis=0)
    twice = [jnp.concatenate([t] * micros, axis=0) for t in (cosine, sine)]
    key_own = rotate(kv_own[:, :size], twice[0], -twice[1])
    kv_grad = jnp.concatenate([key_own, kv_own[:, size:]], axis=1).astype(BF16)

    def narrow_back(kv_grad, normed):
        return contract_rows(normed, kv_grad, BF16)

    def inputs_back(kv_grad, part, weights, tokens, gain, middle_grads):
        attn_in_grad = part + contract_last(kv_grad, weights)
        norm_back = jax.vjp(rms_scale, tokens[:, 0].astype(F32), gain)[1]
        input_part, gain_one = norm_back(attn_in_grad.reshape(micros, rows, width))
        return jnp.stack(middle_grads) + input_part, gain_one

    kv_terms = plan.run(narrow_back, kv_grad, normed)
    grad_tokens, gain_one = plan.run(
        inputs_back, kv_grad, part, w_kv, tokens, gain_first, middle_grads
    )
    gain_cols = jnp.stack([gain_one, sum(gain_two)], axis=1).astype(BF16)
    narrow_out = plan.start(scatter_everywhere(
        jnp.concatenate([kv_terms, jnp.pad(gain_cols, ((0, 0), (0, 126)))], axis=1)
    ))
    for _ in range(count):
        plan.step(narrow_out, out_out, query_out)
    narrow_grad = narrow_out.end()
    return (
        output[:, None],
        grad_tokens[:, None],
        narrow_grad[:, 2 * size],
        query_out.end(),
        narrow_grad[:, :size],
        narrow_grad[:, size : 2 * size],
        out_out.end().T,
        narrow_grad[:, 2 * size + 1],
        gate_out.value.astype(F32),
        up_out.end().astype(F32),
        down_out.value.T.astype(F32),
    )


def solution(mesh):
    rows = P(None, "wt", "ctx", None)
    everywhere = P(("ctx", "wt"))
    tall = P(("ctx", "wt"), None)
    wide = P(None, ("ctx", "wt"))
    square = P("ctx", "wt")
    return jax.shard_map(
        local,
        mesh=mesh,
        in_specs=(
            rows, P(None, "wt", "ctx"), rows, everywhere, tall, tall, tall, wide, everywhere,
            square, square, P("wt", "ctx"),
        ),
        out_specs=(
            rows, rows, everywhere, tall, tall, tall, wide, everywhere, square, square,
            P("wt", "ctx"),
        ),
        check_vma=False,
    )
```
